32 devices in a mesh: row: 4 (over z), col: 8 (over y, x, core).
Axes of the slice: x: 2, y: 2, z: 4, core: 2. Of those that a mesh axis runs over, the one named last changes fastest.
Arguments:
- snapshots: float32 [128, 49152], P(('row', 'col')), may hold values from -6 to 6
- panels: float32 [8, 6, 8192, 256], P(None, None, ('row', 'col')), may hold values from -0.1875 to 0.1875
- diag_inverse: float32 [8, 256, 256], replicated, may hold values from -0.6 to 1.5, as said below
Outputs:
- whitened: float32 [6, 8192, 128], P(None, ('row', 'col'))
The draws below stay inside these ranges and needn't reach their ends.
Inputs may be any that keep to these rules, and one draw needn't show every extreme that they name: Each block of diag_inverse is lower triangular with a diagonal of 0.5 to 1.5.
All inputs are finite; a program needn't handle non-finite values.
Results may differ from the reference program's by a relative error of at most 0.0001.
Values sent between devices are 32-bit elements; how exact they have to be, the bound alone decides.
A program may use at most 128 MiB of HBM per device.

```python
import math
import jax
import jax.numpy as jnp
from jax import lax

NB = 256
STEPS = 8
BLK_DEV = 6
M = 49152
S = 128
DEVICES = 32


def draw_diag_inverse(key, part):
    first_key, second_key = jax.random.split(jax.random.fold_in(key, 17))
    below = jnp.clip(jax.random.normal(first_key, (STEPS, NB, NB), jnp.float32), -4.0, 4.0) * (0.6 / math.sqrt(NB))
    diagonal = jnp.exp(jax.random.uniform(second_key, (STEPS, NB), jnp.float32, math.log(0.5), math.log(1.5)))
    row_index = lax.broadcasted_iota(jnp.int32, (STEPS, NB, NB), 1)
    col_index = lax.broadcasted_iota(jnp.int32, (STEPS, NB, NB), 2)
    return jnp.where(row_index > col_index, below, jnp.where(row_index == col_index, diagonal[:, :, None], 0.0))


def steps_of(rng, shape, cuts, least, top_value):
    def one(dim, blocks):
        heights = jax.random.uniform(jax.random.fold_in(jax.random.fold_in(rng, 6), dim), (blocks,), jnp.float32, least / len(cuts), top_value / len(cuts))
        return jnp.repeat(jnp.exp(heights), shape[dim] // blocks).reshape((-1,) + (1,) * (len(shape) - dim - 1))

    gain = one(*cuts[0])
    for cut in cuts[1:]:
        gain = gain * one(*cut)
    return gain


def normal_values(own_key, extent, spread, limit, cuts=(), kind=jnp.bfloat16):
    array = jax.random.normal(own_key, extent, jnp.float32) * spread
    if len(cuts) > 0:
        array = steps_of(own_key, extent, cuts, -0.22, 0.18) * array
    return jnp.clip(array, min=-limit, max=limit).astype(kind)


def setup_inputs(seed: int = 0) -> dict:
    keys = jax.random.split(jax.random.key(seed), 4)
    snapshots = normal_values(keys[0], (S, M), 1.0, 6.0, ((0, 32),), jnp.float32)
    panels = normal_values(keys[1], (STEPS, BLK_DEV, DEVICES * NB, NB), (4 * NB) ** -0.5, 0.1875, ((2, 32),), jnp.float32)
    diag_inverse = draw_diag_inverse(jax.random.fold_in(keys[3], 71), 0)
    return {"snapshots": snapshots, "panels": panels, "diag_inverse": diag_inverse}


def reference(snapshots, panels, diag_inverse):
    remaining = jnp.transpose(snapshots)
    columns = panels.reshape(panels.shape[0], -1, panels.shape[3])
    row_index = lax.broadcasted_iota(jnp.int32, (remaining.shape[0], 1), 0)
    for section in range(STEPS):
        offset = section * NB
        leading = remaining[offset:offset + NB]
        solved = jnp.dot(diag_inverse[section], leading, precision=lax.Precision.HIGHEST, preferred_element_type=jnp.float32)
        product = jnp.dot(columns[section], solved, precision=lax.Precision.HIGHEST, preferred_element_type=jnp.float32)
        remaining = jnp.where(row_index >= offset + NB, remaining - product, remaining)
        remaining = remaining.at[offset:offset + NB].set(solved)
    return remaining.reshape(BLK_DEV, -1, remaining.shape[1])
```

```python
import functools

import jax
import jax.numpy as jnp
from jax import lax
from jax.experimental import pallas as pl
from jax.experimental.pallas import tpu as pltpu
from jax.sharding import PartitionSpec as P

MESH = pl.DeviceIdType.MESH
NT = (((1,), (1,)), ((), ()))
NN = (((1,), (0,)), ((), ()))


def halves(value):
    high = value.astype(jnp.bfloat16)
    low = (value - high.astype(jnp.float32)).astype(jnp.bfloat16)
    return high, low


def mul(a, b, dims):
    return lax.dot_general(a, b, dims, preferred_element_type=jnp.float32)


def product(a, b_high, b_low, dims):
    rows = a.shape[0]
    a_high, a_low = halves(a)
    both = mul(jnp.concatenate([a_high, a_low], axis=0), b_high, dims)
    return both[:rows] + (both[rows:] + mul(a_high, b_low, dims))


def kernel(
    rows, cols, snap, panels, diag, out,
    recv, first, solved, strip, strip_high, strip_low, inverse_high, inverse_low,
    diagonal, lead, staged, high, low, both, total, piled,
    a2a_send, a2a_recv, first_send, first_recv, strip_send, strip_recv, strip_own, diag_sem,
    staged_sem, half_send, half_recv, partner_send, up_send, piece_recv, plane_send,
):
    devices = rows * cols
    groups = cols // 2
    steps, blocks, width, _ = panels.shape
    stages = steps // 2
    count = out.shape[2]
    half_count = count // 2
    local = snap.shape[3]
    half_devices = devices // 2

    row = lax.axis_index("row")
    col = lax.axis_index("col")
    me = row * cols + col
    group = col // 2
    side = col % 2
    in_chain = me < steps

    def device(index):
        return (index // cols, index % cols)

    def remote(src, dst, send, recv_sem, target):
        return pltpu.make_async_remote_copy(
            src_ref=src, dst_ref=dst, send_sem=send, recv_sem=recv_sem,
            device_id=target, device_id_type=MESH,
        )

    def arrived(ref, sem):
        pltpu.make_async_copy(ref, ref, sem).wait()

    def strip_local(k):
        return pltpu.make_async_copy(panels.at[k, 0], strip.at[side, k], strip_own.at[k])

    def diag_copy():
        return pltpu.make_async_copy(diag.at[pl.ds(2 * group, 2)], diagonal, diag_sem)

    def staged_copy(k):
        return pltpu.make_async_copy(panels.at[k], staged.at[k], staged_sem.at[k])

    @pl.when(in_chain)
    def _():
        diag_copy().start()
        for k in range(steps - 1):
            @pl.when(k < me)
            def _():
                strip_local(k).start()

    for k in range(steps):
        staged_copy(k).start()

    barrier = pltpu.get_barrier_semaphore()

    def greet(i, carry):
        pl.semaphore_signal(
            barrier, inc=1, device_id=device((me + i) % devices), device_id_type=MESH
        )
        return carry

    lax.fori_loop(1, devices, greet, 0)
    pl.semaphore_wait(barrier, devices - 1)

    my_half = me // half_devices
    place = me % half_devices

    def first_remote(c):
        return remote(
            snap.at[0, pl.ds(2 * c, 2)], first.at[place], first_send.at[c],
            first_recv.at[place], device(2 * c + my_half),
        )

    def first_local(c):
        return pltpu.make_async_copy(
            snap.at[0, pl.ds(2 * c, 2)], first.at[place], first_recv.at[place]
        )

    for c in range(stages):
        @pl.when(2 * c + my_half != me)
        def _():
            first_remote(c).start()

        @pl.when(2 * c + my_half == me)
        def _():
            first_local(c).start()

    partner = (row, 2 * group + 1 - side)

    def strip_remote(k):
        return remote(
            panels.at[k, 0], strip.at[side, k], strip_send.at[k], strip_recv.at[k], partner
        )

    @pl.when(in_chain)
    def _():
        for k in reversed(range(steps - 1)):
            @pl.when(k < me)
            def _():
                strip_remote(k).start()

    def a2a_lead(target):
        return remote(
            snap.at[pl.ds(1, blocks - 1), target], recv.at[me, pl.ds(1, blocks - 1)],
            a2a_send.at[target], a2a_recv.at[me], device(target),
        )

    def a2a_rest(target):
        return remote(
            snap.at[:, target], recv.at[me], a2a_send.at[target], a2a_recv.at[me], device(target)
        )

    def a2a_start(i, carry):
        target = (me + i) % devices

        @pl.when(target < steps)
        def _():
            a2a_lead(target).start()

        @pl.when(target >= steps)
        def _():
            a2a_rest(target).start()

        return carry

    lax.fori_loop(1, devices, a2a_start, 0)
    own_copy = pltpu.make_async_copy(snap.at[:, me], recv.at[me], a2a_recv.at[me])
    own_copy.start()

    def split_all():
        for k in range(steps):
            staged_copy(k).wait()

        def one(i, carry):
            s, j = i // blocks, i % blocks
            for t in range(2):
                h, l = halves(staged[2 * s + t, j])
                high[s, j, :, t * width:(t + 1) * width] = h
                low[s, j, :, t * width:(t + 1) * width] = l
            return carry

        lax.fori_loop(0, stages * blocks, one, 0)

    early = jnp.logical_or(me >= steps, me >= steps // 2)

    def half_ref(s, which):
        return solved.at[s, pl.ds(which * groups, groups)]

    mine = side * groups + group

    def to_partner(s):
        return remote(
            half_ref(s, side), half_ref(s, side), partner_send.at[s],
            half_recv.at[s, side], partner,
        )

    def upward(s, r):
        return remote(
            solved.at[s, mine], solved.at[s, mine], up_send.at[s, r - 1],
            piece_recv.at[s, mine], (r, col),
        )

    def forward(s):
        for r in range(1, rows):
            upward(s, r).start()
        to_partner(s).start()

    def across(s, g):
        return remote(
            half_ref(s, side), half_ref(s, side), half_send.at[g],
            half_recv.at[s, side], (row, 2 * g + side),
        )

    def in_plane(s, i):
        target = (col + i) % cols
        return remote(
            solved.at[s, mine], solved.at[s, mine], plane_send.at[s, i - 1],
            piece_recv.at[s, mine], (row, target),
        )

    @pl.when(early)
    def _():
        split_all()

    @pl.when(in_chain)
    def _():
        diag_copy().wait()
        for k in range(steps - 1):
            @pl.when(k < me)
            def _():
                strip_local(k).wait()

            @pl.when(k < 2 * group + 1 - side)
            def _():
                arrived(strip.at[1 - side, k], strip_recv.at[k])

        d0, d1 = diagonal[0], diagonal[1]
        d0_high, d0_low = halves(d0)
        below = strip[1, 2 * group]
        inner = product(below, d0_high, d0_low, NN)
        inner_high, inner_low = halves(inner)
        corner = -product(d1, inner_high, inner_low, NN)
        for r0, c0, value in (
            (0, 0, d0), (0, width, jnp.zeros_like(d0)), (width, 0, corner), (width, width, d1)
        ):
            h, l = halves(value)
            inverse_high[r0:r0 + width, c0:c0 + width] = h
            inverse_low[r0:r0 + width, c0:c0 + width] = l
        for s in range(stages - 1):
            @pl.when(s < group)
            def _():
                for b in range(2):
                    for t in range(2):
                        h, l = halves(strip[b, 2 * s + t])
                        place_ = (s, slice(b * width, (b + 1) * width), slice(t * width, (t + 1) * width))
                        strip_high[place_] = h
                        strip_low[place_] = l

        def first_wait(i, carry):
            arrived(first.at[i], first_recv.at[i])
            return carry

        lax.fori_loop(0, half_devices, first_wait, 0)

        def pile(i, carry):
            at = pl.ds(pl.multiple_of(i * 2 * local, 2 * local), 2 * local)
            for b in range(2):
                for t in range(width // 128):
                    lanes = slice(b * width + t * 128, b * width + (t + 1) * 128)
                    lead[at, lanes] = jnp.concatenate(
                        [first[2 * i, b, t], first[2 * i + 1, b, t]], axis=0
                    )
            return carry

        lax.fori_loop(0, half_devices // 2, pile, 0)

        for s in range(stages):
            @pl.when(s < group)
            def _():
                arrived(half_ref(s, side), half_recv.at[s, side])
                forward(s)
                x = half_ref(s, side)[...].reshape(half_count, 2 * width)
                lead[...] -= product(x, strip_high[min(s, stages - 2)], strip_low[min(s, stages - 2)], NT)

            @pl.when(s == group)
            def _():
                x = product(lead[...], inverse_high[...], inverse_low[...], NT)
                half_ref(s, side)[...] = x.reshape(groups, half_count // groups, 2 * width)
                for i in range(1, groups):
                    across(s, (s + i) % groups).start()
                forward(s)

    @pl.when(jnp.logical_not(early))
    def _():
        split_all()

    for s in range(stages):
        @pl.when(row == 0)
        def _():
            @pl.when(jnp.logical_or(jnp.logical_not(in_chain), s > group))
            def _():
                arrived(half_ref(s, side), half_recv.at[s, side])
                forward(s)

            arrived(half_ref(s, 1 - side), half_recv.at[s, 1 - side])

        @pl.when(row > 0)
        def _():
            arrived(solved.at[s, mine], piece_recv.at[s, mine])
            for i in range(1, cols):
                in_plane(s, i).start()
            for i in range(1, cols):
                other = (col + i) % cols
                piece = (other % 2) * groups + other // 2
                arrived(solved.at[s, piece], piece_recv.at[s, piece])

        x_high, x_low = halves(solved[s].reshape(count, 2 * width))
        both[:count] = x_high
        both[count:] = x_low

        def update(j, carry):
            a = mul(high[s, j], both[...], NT)
            b = mul(low[s, j], both[:count], NT)
            term = a[:, :count] + (a[:, count:] + b)
            if s == 0:
                total[j] = term
            else:
                total[j] += term
            return carry

        lax.fori_loop(0, blocks, update, 0)

    own_copy.wait()

    def a2a_wait(i, carry):
        source = (me + i) % devices

        @pl.when(in_chain)
        def _():
            arrived(recv.at[source, pl.ds(1, blocks - 1)], a2a_recv.at[source])

        @pl.when(jnp.logical_not(in_chain))
        def _():
            arrived(recv.at[source], a2a_recv.at[source])

        return carry

    lax.fori_loop(1, devices, a2a_wait, 0)

    def finish(j):
        def pile(i, carry):
            at = pl.ds(pl.multiple_of(i * 2 * local, 2 * local), 2 * local)
            for t in range(width // 128):
                piled[t, at] = jnp.concatenate([recv[2 * i, j, t], recv[2 * i + 1, j, t]], axis=0)
            return carry

        lax.fori_loop(0, half_devices, pile, 0)
        for t in range(width // 128):
            at = slice(t * 128, (t + 1) * 128)
            out[j, at] = piled[t].T - total[j, at]

    @pl.when(in_chain)
    def _():
        for s in range(stages):
            for t in range(2):
                @pl.when(me == 2 * s + t)
                def _():
                    x = solved[s].reshape(count, 2 * width)
                    out[0] = x[:, t * width:(t + 1) * width].T

    @pl.when(jnp.logical_not(in_chain))
    def _():
        finish(0)

    for j in range(1, blocks):
        finish(j)

    for c in range(stages):
        @pl.when(2 * c + my_half != me)
        def _():
            first_remote(c).wait_send()

    @pl.when(in_chain)
    def _():
        for k in range(steps - 1):
            @pl.when(k < me)
            def _():
                strip_remote(k).wait_send()
        for s in range(stages):
            @pl.when(s == group)
            def _():
                for i in range(1, groups):
                    across(s, (s + i) % groups).wait_send()

    def a2a_sent(i, carry):
        target = (me + i) % devices

        @pl.when(target < steps)
        def _():
            a2a_lead(target).wait_send()

        @pl.when(target >= steps)
        def _():
            a2a_rest(target).wait_send()

        return carry

    lax.fori_loop(1, devices, a2a_sent, 0)
    for s in range(stages):
        @pl.when(row == 0)
        def _():
            to_partner(s).wait_send()
            for r in range(1, rows):
                upward(s, r).wait_send()

        @pl.when(row > 0)
        def _():
            for i in range(1, cols):
                in_plane(s, i).wait_send()


def per_device(rows, cols, snapshots, panels, diag_inverse):
    local, order = snapshots.shape
    steps, blocks, width, _ = panels.shape
    devices = rows * cols
    groups = cols // 2
    stages = steps // 2
    count = local * devices
    lanes = 128
    snap = snapshots.reshape(local, blocks, devices, width // lanes, lanes).transpose(1, 2, 3, 0, 4)
    f32, bf16 = jnp.float32, jnp.bfloat16
    vmem, dma = pltpu.VMEM, pltpu.SemaphoreType.DMA
    return pl.pallas_call(
        functools.partial(kernel, rows, cols),
        out_shape=jax.ShapeDtypeStruct((blocks, width, count), f32),
        in_specs=[pl.BlockSpec(memory_space=pl.ANY)] * 3,
        out_specs=pl.BlockSpec(memory_space=pltpu.VMEM),
        scratch_shapes=[
            vmem((devices, blocks, width // lanes, local, lanes), f32),
            vmem((devices // 2, 2, width // lanes, local, lanes), f32),
            vmem((stages, cols, count // cols, 2 * width), f32),
            vmem((2, steps, width, width), f32),
            vmem((stages - 1, 2 * width, 2 * width), bf16),
            vmem((stages - 1, 2 * width, 2 * width), bf16),
            vmem((2 * width, 2 * width), bf16),
            vmem((2 * width, 2 * width), bf16),
            vmem((2, width, width), f32),
            vmem((count // 2, 2 * width), f32),
            vmem((steps, blocks, width, width), f32),
            vmem((stages, blocks, width, 2 * width), bf16),
            vmem((stages, blocks, width, 2 * width), bf16),
            vmem((2 * count, 2 * width), bf16),
            vmem((blocks, width, count), f32),
            vmem((width // lanes, count, lanes), f32),
            dma((devices,)), dma((devices,)),
            dma((stages,)), dma((devices // 2,)),
            dma((steps,)), dma((steps,)), dma((steps,)), dma(()),
            dma((steps,)),
            dma((groups,)), dma((stages, 2)), dma((stages,)), dma((stages, rows - 1)),
            dma((stages, cols)), dma((stages, cols - 1)),
        ],
        compiler_params=pltpu.CompilerParams(
            collective_id=0, has_side_effects=True, vmem_limit_bytes=58 * 1024 * 1024
        ),
        cost_estimate=pl.CostEstimate(
            flops=6 * steps * blocks * width * width * count,
            bytes_accessed=4 * steps * blocks * width * width,
            transcendentals=0,
        ),
    )(snap, panels, diag_inverse)


def solution(mesh):
    in_specs = (P(("row", "col"), None), P(None, None, ("row", "col"), None), P())
    out_specs = P(None, ("row", "col"), None)
    body = functools.partial(per_device, mesh.shape["row"], mesh.shape["col"])
    return jax.shard_map(
        body, mesh=mesh, in_specs=in_specs, out_specs=out_specs, check_vma=False
    )
```

```python
import functools

import jax
import jax.numpy as jnp
from jax import lax
from jax.experimental import pallas as pl
from jax.experimental.pallas import tpu as pltpu
from jax.sharding import PartitionSpec as P

MESH = pl.DeviceIdType.MESH
NT = (((1,), (1,)), ((), ()))
NN = (((1,), (0,)), ((), ()))


def halves(value):
    high = value.astype(jnp.bfloat16)
    low = (value - high.astype(jnp.float32)).astype(jnp.bfloat16)
    return high, low


def mul(a, b, dims):
    return lax.dot_general(a, b, dims, preferred_element_type=jnp.float32)


def product(a, b_high, b_low, dims):
    rows = a.shape[0]
    a_high, a_low = halves(a)
    both = mul(jnp.concatenate([a_high, a_low], axis=0), b_high, dims)
    return both[:rows] + (both[rows:] + mul(a_high, b_low, dims))


def kernel(
    rows, cols, snap, panels, diag, out,
    recv, first, solved, strip, strip_high, strip_low, inverse_high, inverse_low,
    diagonal, lead, staged, high, low, both, total, piled,
    a2a_send, a2a_recv, first_send, first_recv, strip_send, strip_recv, strip_own, diag_sem,
    staged_sem, half_send, half_recv, partner_send, up_send, piece_recv, plane_send,
):
    devices = rows * cols
    groups = cols // 2
    steps, blocks, width, _ = panels.shape
    stages = steps // 2
    count = out.shape[2]
    half_count = count // 2
    local = snap.shape[3]
    half_devices = devices // 2

    row = lax.axis_index("row")
    col = lax.axis_index("col")
    me = row * cols + col
    group = col // 2
    side = col % 2
    in_chain = me < steps

    def device(index):
        return (index // cols, index % cols)

    def remote(src, dst, send, recv_sem, target):
        return pltpu.make_async_remote_copy(
            src_ref=src, dst_ref=dst, send_sem=send, recv_sem=recv_sem,
            device_id=target, device_id_type=MESH,
        )

    def arrived(ref, sem):
        pltpu.make_async_copy(ref, ref, sem).wait()

    def strip_local(k):
        return pltpu.make_async_copy(panels.at[k, 0], strip.at[side, k], strip_own.at[k])

    def diag_copy():
        return pltpu.make_async_copy(diag.at[pl.ds(2 * group, 2)], diagonal, diag_sem)

    def staged_copy(k):
        return pltpu.make_async_copy(panels.at[k], staged.at[k], staged_sem.at[k])

    @pl.when(in_chain)
    def _():
        diag_copy().start()
        for k in range(steps - 1):
            @pl.when(k < me)
            def _():
                strip_local(k).start()

    barrier = pltpu.get_barrier_semaphore()

    def greet(i, carry):
        pl.semaphore_signal(
            barrier, inc=1, device_id=device((me + i) % devices), device_id_type=MESH
        )
        return carry

    lax.fori_loop(1, devices, greet, 0)
    pl.semaphore_wait(barrier, devices - 1)

    my_half = me // half_devices
    place = me % half_devices

    def first_remote(c):
        return remote(
            snap.at[0, pl.ds(2 * c, 2)], first.at[place], first_send.at[c],
            first_recv.at[place], device(2 * c + my_half),
        )

    def first_local(c):
        return pltpu.make_async_copy(
            snap.at[0, pl.ds(2 * c, 2)], first.at[place], first_recv.at[place]
        )

    for c in range(stages):
        @pl.when(2 * c + my_half != me)
        def _():
            first_remote(c).start()

        @pl.when(2 * c + my_half == me)
        def _():
            first_local(c).start()

    partner = (row, 2 * group + 1 - side)

    def strip_remote(k):
        return remote(
            panels.at[k, 0], strip.at[side, k], strip_send.at[k], strip_recv.at[k], partner
        )

    @pl.when(in_chain)
    def _():
        for k in reversed(range(steps - 1)):
            @pl.when(k < me)
            def _():
                strip_remote(k).start()

    for k in range(steps):
        staged_copy(k).start()

    def a2a_lead(target):
        return remote(
            snap.at[pl.ds(1, blocks - 1), target], recv.at[me, pl.ds(1, blocks - 1)],
            a2a_send.at[target], a2a_recv.at[me], device(target),
        )

    def a2a_rest(target):
        return remote(
            snap.at[:, target], recv.at[me], a2a_send.at[target], a2a_recv.at[me], device(target)
        )

    def a2a_start(i, carry):
        target = (me + 1 + (i + devices // 2 - cols // 2) % (devices - 1)) % devices

        @pl.when(target < steps)
        def _():
            a2a_lead(target).start()

        @pl.when(target >= steps)
        def _():
            a2a_rest(target).start()

        return carry

    def send_rest():
        lax.fori_loop(0, devices - 1, a2a_start, 0)

    first_group = jnp.logical_and(in_chain, group == 0)

    @pl.when(jnp.logical_not(first_group))
    def _():
        send_rest()

    own_copy = pltpu.make_async_copy(snap.at[:, me], recv.at[me], a2a_recv.at[me])
    own_copy.start()

    def split_all():
        for k in range(steps):
            staged_copy(k).wait()

        def one(i, carry):
            s, j = i // blocks, i % blocks
            for t in range(2):
                h, l = halves(staged[2 * s + t, j])
                high[s, j, :, t * width:(t + 1) * width] = h
                low[s, j, :, t * width:(t + 1) * width] = l
            return carry

        lax.fori_loop(0, stages * blocks, one, 0)

    early = jnp.logical_or(me >= steps, me >= steps // 2)

    def half_ref(s, which):
        return solved.at[s, pl.ds(which * groups, groups)]

    mine = side * groups + group

    def full(s, g):
        return jnp.logical_and(g > s, g < stages)

    def to_partner(s, q):
        piece = side * groups + q
        return remote(
            solved.at[s, piece], solved.at[s, piece], partner_send.at[s, q],
            piece_recv.at[s, piece], partner,
        )

    def upward(s, r):
        return remote(
            solved.at[s, mine], solved.at[s, mine], up_send.at[s, r - 1],
            piece_recv.at[s, mine], (r, col),
        )

    def in_plane(s, i):
        g = (group + i) % groups
        return remote(
            solved.at[s, mine], solved.at[s, mine], plane_send.at[s, i - 1],
            piece_recv.at[s, mine], (row, 2 * g + side),
        )

    def own_piece(s, act):
        @pl.when(row == 0)
        def _():
            for r in range(1, rows):
                act(upward(s, r))

        for i in range(1, groups):
            g = (group + i) % groups
            has = jnp.logical_or(full(s, g), g == s)

            @pl.when(jnp.logical_not(jnp.logical_and(row == 0, has)))
            def _():
                act(in_plane(s, i))

    def forward(s):
        own_piece(s, lambda copy: copy.start())
        for q in range(groups):
            to_partner(s, q).start()

    def across(s, i, act):
        g = (s + i) % groups
        if s < g < stages:
            act(remote(
                half_ref(s, side), half_ref(s, side), half_send.at[i - 1],
                half_recv.at[s, side], (row, 2 * g + side),
            ))
        else:
            piece = side * groups + g
            act(remote(
                solved.at[s, piece], solved.at[s, piece], half_send.at[i - 1],
                piece_recv.at[s, piece], (row, 2 * g + side),
            ))

    @pl.when(early)
    def _():
        split_all()

    @pl.when(in_chain)
    def _():
        diag_copy().wait()
        for k in range(steps - 1):
            @pl.when(k < me)
            def _():
                strip_local(k).wait()

            @pl.when(k < 2 * group + 1 - side)
            def _():
                arrived(strip.at[1 - side, k], strip_recv.at[k])

        d0, d1 = diagonal[0], diagonal[1]
        d0_high, d0_low = halves(d0)
        below = strip[1, 2 * group]
        inner = product(below, d0_high, d0_low, NN)
        inner_high, inner_low = halves(inner)
        corner = -product(d1, inner_high, inner_low, NN)
        for r0, c0, value in (
            (0, 0, d0), (0, width, jnp.zeros_like(d0)), (width, 0, corner), (width, width, d1)
        ):
            h, l = halves(value)
            inverse_high[r0:r0 + width, c0:c0 + width] = h
            inverse_low[r0:r0 + width, c0:c0 + width] = l
        for s in range(stages - 1):
            @pl.when(s < group)
            def _():
                for b in range(2):
                    for t in range(2):
                        h, l = halves(strip[b, 2 * s + t])
                        place_ = (s, slice(b * width, (b + 1) * width), slice(t * width, (t + 1) * width))
                        strip_high[place_] = h
                        strip_low[place_] = l

        def first_wait(i, carry):
            arrived(first.at[i], first_recv.at[i])
            return carry

        lax.fori_loop(0, half_devices, first_wait, 0)

        def pile(i, carry):
            at = pl.ds(pl.multiple_of(i * 2 * local, 2 * local), 2 * local)
            for b in range(2):
                for t in range(width // 128):
                    lanes = slice(b * width + t * 128, b * width + (t + 1) * 128)
                    lead[at, lanes] = jnp.concatenate(
                        [first[2 * i, b, t], first[2 * i + 1, b, t]], axis=0
                    )
            return carry

        lax.fori_loop(0, half_devices // 2, pile, 0)

        for s in range(stages):
            @pl.when(s < group)
            def _():
                arrived(half_ref(s, side), half_recv.at[s, side])

                @pl.when(s + 1 < group)
                def _():
                    forward(s)

                x = half_ref(s, side)[...].reshape(half_count, 2 * width)
                lead[...] -= product(x, strip_high[min(s, stages - 2)], strip_low[min(s, stages - 2)], NT)

            @pl.when(s == group)
            def _():
                x = product(lead[...], inverse_high[...], inverse_low[...], NT)
                half_ref(s, side)[...] = x.reshape(groups, half_count // groups, 2 * width)
                for i in range(1, groups):
                    across(s, i, lambda copy: copy.start())
                if s > 0:
                    forward(s - 1)
                forward(s)
                if s == 0:
                    send_rest()

    @pl.when(jnp.logical_not(early))
    def _():
        split_all()

    def update_with(s):
        holds = jnp.logical_and(row == 0, jnp.logical_and(in_chain, s <= group))

        @pl.when(jnp.logical_not(holds))
        def _():
            arrived(solved.at[s, mine], piece_recv.at[s, mine])
            own_piece(s, lambda copy: copy.start())
            to_partner(s, group).start()
            for i in range(1, groups):
                q = (group + i) % groups
                piece = side * groups + q
                arrived(solved.at[s, piece], piece_recv.at[s, piece])
                to_partner(s, q).start()

        for q in range(groups):
            piece = (1 - side) * groups + q
            arrived(solved.at[s, piece], piece_recv.at[s, piece])

        x_high, x_low = halves(solved[s].reshape(count, 2 * width))
        both[:count] = x_high
        both[count:] = x_low

        def update(j, carry):
            a = mul(high[s, j], both[...], NT)
            b = mul(low[s, j], both[:count], NT)
            term = a[:, :count] + (a[:, count:] + b)
            if s == 0:
                total[j] = term
            elif s < stages - 1:
                total[j] += term
            else:
                out[j] -= term
            return carry

        lax.fori_loop(0, blocks, update, 0)

    for s in range(stages - 1):
        update_with(s)

    own_copy.wait()

    def a2a_wait(i, carry):
        source = (me + i) % devices

        @pl.when(in_chain)
        def _():
            arrived(recv.at[source, pl.ds(1, blocks - 1)], a2a_recv.at[source])

        @pl.when(jnp.logical_not(in_chain))
        def _():
            arrived(recv.at[source], a2a_recv.at[source])

        return carry

    lax.fori_loop(1, devices, a2a_wait, 0)

    def finish(j):
        def pile(i, carry):
            at = pl.ds(pl.multiple_of(i * 2 * local, 2 * local), 2 * local)
            for t in range(width // 128):
                piled[t, at] = jnp.concatenate([recv[2 * i, j, t], recv[2 * i + 1, j, t]], axis=0)
            return carry

        lax.fori_loop(0, half_devices, pile, 0)
        for t in range(width // 128):
            at = slice(t * 128, (t + 1) * 128)
            out[j, at] = piled[t].T - total[j, at]

    @pl.when(jnp.logical_not(in_chain))
    def _():
        finish(0)

    @pl.when(in_chain)
    def _():
        out[0] = jnp.zeros_like(out[0])

    for j in range(1, blocks):
        finish(j)

    update_with(stages - 1)

    @pl.when(in_chain)
    def _():
        for s in range(stages):
            for t in range(2):
                @pl.when(me == 2 * s + t)
                def _():
                    x = solved[s].reshape(count, 2 * width)
                    out[0] = x[:, t * width:(t + 1) * width].T

    for c in range(stages):
        @pl.when(2 * c + my_half != me)
        def _():
            first_remote(c).wait_send()

    @pl.when(in_chain)
    def _():
        for k in range(steps - 1):
            @pl.when(k < me)
            def _():
                strip_remote(k).wait_send()
        for s in range(stages):
            @pl.when(s == group)
            def _():
                for i in range(1, groups):
                    across(s, i, lambda copy: copy.wait_send())

    def a2a_sent(i, carry):
        target = (me + i) % devices

        @pl.when(target < steps)
        def _():
            a2a_lead(target).wait_send()

        @pl.when(target >= steps)
        def _():
            a2a_rest(target).wait_send()

        return carry

    lax.fori_loop(1, devices, a2a_sent, 0)
    for s in range(stages):
        own_piece(s, lambda copy: copy.wait_send())
        for q in range(groups):
            to_partner(s, q).wait_send()


def per_device(rows, cols, snapshots, panels, diag_inverse):
    local, order = snapshots.shape
    steps, blocks, width, _ = panels.shape
    devices = rows * cols
    groups = cols // 2
    stages = steps // 2
    count = local * devices
    lanes = 128
    snap = snapshots.reshape(local, blocks, devices, width // lanes, lanes).transpose(1, 2, 3, 0, 4)
    f32, bf16 = jnp.float32, jnp.bfloat16
    vmem, dma = pltpu.VMEM, pltpu.SemaphoreType.DMA
    return pl.pallas_call(
        functools.partial(kernel, rows, cols),
        out_shape=jax.ShapeDtypeStruct((blocks, width, count), f32),
        in_specs=[pl.BlockSpec(memory_space=pl.ANY)] * 3,
        out_specs=pl.BlockSpec(memory_space=pltpu.VMEM),
        scratch_shapes=[
            vmem((devices, blocks, width // lanes, local, lanes), f32),
            vmem((devices // 2, 2, width // lanes, local, lanes), f32),
            vmem((stages, cols, count // cols, 2 * width), f32),
            vmem((2, steps, width, width), f32),
            vmem((stages - 1, 2 * width, 2 * width), bf16),
            vmem((stages - 1, 2 * width, 2 * width), bf16),
            vmem((2 * width, 2 * width), bf16),
            vmem((2 * width, 2 * width), bf16),
            vmem((2, width, width), f32),
            vmem((count // 2, 2 * width), f32),
            vmem((steps, blocks, width, width), f32),
            vmem((stages, blocks, width, 2 * width), bf16),
            vmem((stages, blocks, width, 2 * width), bf16),
            vmem((2 * count, 2 * width), bf16),
            vmem((blocks, width, count), f32),
            vmem((width // lanes, count, lanes), f32),
            dma((devices,)), dma((devices,)),
            dma((stages,)), dma((devices // 2,)),
            dma((steps,)), dma((steps,)), dma((steps,)), dma(()),
            dma((steps,)),
            dma((groups,)), dma((stages, 2)), dma((stages, groups)), dma((stages, rows - 1)),
            dma((stages, cols)), dma((stages, groups - 1)),
        ],
        compiler_params=pltpu.CompilerParams(
            collective_id=0, has_side_effects=True, vmem_limit_bytes=58 * 1024 * 1024
        ),
        cost_estimate=pl.CostEstimate(
            flops=6 * steps * blocks * width * width * count,
            bytes_accessed=4 * steps * blocks * width * width,
            transcendentals=0,
        ),
    )(snap, panels, diag_inverse)


def solution(mesh):
    in_specs = (P(("row", "col"), None), P(None, None, ("row", "col"), None), P())
    out_specs = P(None, ("row", "col"), None)
    body = functools.partial(per_device, mesh.shape["row"], mesh.shape["col"])
    return jax.shard_map(
        body, mesh=mesh, in_specs=in_specs, out_specs=out_specs, check_vma=False
    )
```

```python
import functools

import jax
import jax.numpy as jnp
from jax import lax
from jax.experimental import pallas as pl
from jax.experimental.pallas import tpu as pltpu
from jax.sharding import PartitionSpec as P

MESH = pl.DeviceIdType.MESH
NT = (((1,), (1,)), ((), ()))
NN = (((1,), (0,)), ((), ()))


def halves(value):
    high = value.astype(jnp.bfloat16)
    low = (value - high.astype(jnp.float32)).astype(jnp.bfloat16)
    return high, low


def mul(a, b, dims):
    return lax.dot_general(a, b, dims, preferred_element_type=jnp.float32)


def product(a, b_high, b_low, dims):
    rows = a.shape[0]
    a_high, a_low = halves(a)
    both = mul(jnp.concatenate([a_high, a_low], axis=0), b_high, dims)
    return both[:rows] + (both[rows:] + mul(a_high, b_low, dims))


def kernel(
    rows, cols, snap, panels, diag, out,
    packed, recv, first, solved, strip, strip_high, strip_low, inverse_high, inverse_low,
    diagonal, lead, staged, high, low, both, total, piled,
    a2a_send, a2a_recv, first_send, first_recv, strip_send, strip_recv, strip_own, diag_sem,
    staged_sem, half_send, half_recv, partner_send, up_send, piece_recv, plane_send,
    pack_sem,
):
    devices = rows * cols
    groups = cols // 2
    steps, blocks, width, _ = panels.shape
    stages = steps // 2
    count = out.shape[2]
    half_count = count // 2
    local = snap.shape[3]
    half_devices = devices // 2

    row = lax.axis_index("row")
    col = lax.axis_index("col")
    me = row * cols + col
    group = col // 2
    side = col % 2
    in_chain = me < steps

    def device(index):
        return (index // cols, index % cols)

    def remote(src, dst, send, recv_sem, target):
        return pltpu.make_async_remote_copy(
            src_ref=src, dst_ref=dst, send_sem=send, recv_sem=recv_sem,
            device_id=target, device_id_type=MESH,
        )

    def arrived(ref, sem):
        pltpu.make_async_copy(ref, ref, sem).wait()

    def strip_local(k):
        return pltpu.make_async_copy(panels.at[k, 0], strip.at[side, k], strip_own.at[k])

    def diag_copy():
        return pltpu.make_async_copy(diag.at[pl.ds(2 * group, 2)], diagonal, diag_sem)

    def staged_copy(k):
        return pltpu.make_async_copy(panels.at[k], staged.at[k], staged_sem.at[k])

    def pack(j):
        return pltpu.make_async_copy(snap.at[j], packed.at[:, j], pack_sem.at[j])

    for j in range(blocks):
        pack(j).start()

    @pl.when(in_chain)
    def _():
        diag_copy().start()
        for k in range(steps - 1):
            @pl.when(k < me)
            def _():
                strip_local(k).start()

    barrier = pltpu.get_barrier_semaphore()

    def greet(i, carry):
        pl.semaphore_signal(
            barrier, inc=1, device_id=device((me + i) % devices), device_id_type=MESH
        )
        return carry

    lax.fori_loop(1, devices, greet, 0)
    for j in range(blocks):
        pack(j).wait()
    pl.semaphore_wait(barrier, devices - 1)

    my_half = me // half_devices
    place = me % half_devices

    def first_remote(c):
        return remote(
            packed.at[pl.ds(2 * c, 2), 0], first.at[place], first_send.at[c],
            first_recv.at[place], device(2 * c + my_half),
        )

    def first_local(c):
        return pltpu.make_async_copy(
            packed.at[pl.ds(2 * c, 2), 0], first.at[place], first_recv.at[place]
        )

    for c in range(stages):
        @pl.when(2 * c + my_half != me)
        def _():
            first_remote(c).start()

        @pl.when(2 * c + my_half == me)
        def _():
            first_local(c).start()

    partner = (row, 2 * group + 1 - side)

    def strip_remote(k):
        return remote(
            panels.at[k, 0], strip.at[side, k], strip_send.at[k], strip_recv.at[k], partner
        )

    @pl.when(in_chain)
    def _():
        for k in reversed(range(steps - 1)):
            @pl.when(k < me)
            def _():
                strip_remote(k).start()

    for k in range(steps):
        staged_copy(k).start()

    def a2a_lead(target):
        return remote(
            packed.at[target, pl.ds(1, blocks - 1)], recv.at[me, pl.ds(1, blocks - 1)],
            a2a_send.at[target], a2a_recv.at[me], device(target),
        )

    def a2a_rest(target):
        return remote(
            packed.at[target], recv.at[me], a2a_send.at[target], a2a_recv.at[me], device(target)
        )

    def a2a_start(i, carry):
        target = (me + 1 + (i + devices // 2 - cols // 2) % (devices - 1)) % devices

        @pl.when(target < steps)
        def _():
            a2a_lead(target).start()

        @pl.when(target >= steps)
        def _():
            a2a_rest(target).start()

        return carry

    def send_rest():
        lax.fori_loop(0, devices - 1, a2a_start, 0)

    waiting = me < steps // 2

    @pl.when(jnp.logical_not(waiting))
    def _():
        send_rest()

    own_copy = pltpu.make_async_copy(packed.at[me], recv.at[me], a2a_recv.at[me])
    own_copy.start()

    def split_all():
        for k in range(steps):
            staged_copy(k).wait()

        def one(i, carry):
            s, j = i // blocks, i % blocks
            for t in range(2):
                h, l = halves(staged[2 * s + t, j])
                high[s, j, :, t * width:(t + 1) * width] = h
                low[s, j, :, t * width:(t + 1) * width] = l
            return carry

        lax.fori_loop(0, stages * blocks, one, 0)

    early = jnp.logical_or(me >= steps, me >= steps // 2)

    def half_ref(s, which):
        return solved.at[s, pl.ds(which * groups, groups)]

    mine = side * groups + group

    def full(s, g):
        return jnp.logical_and(g > s, g < stages)

    def to_partner(s, q):
        piece = side * groups + q
        return remote(
            solved.at[s, piece], solved.at[s, piece], partner_send.at[s, q],
            piece_recv.at[s, piece], partner,
        )

    def upward(s):
        return remote(
            solved.at[s, mine], solved.at[s, mine], up_send.at[s],
            piece_recv.at[s, mine], (row + 1, col),
        )

    def in_plane(s, i):
        g = (group + i) % groups
        return remote(
            solved.at[s, mine], solved.at[s, mine], plane_send.at[s, i - 1],
            piece_recv.at[s, mine], (row, 2 * g + side),
        )

    def own_piece(s, act):
        @pl.when(row < rows - 1)
        def _():
            act(upward(s))

        for i in range(1, groups):
            g = (group + i) % groups
            has = jnp.logical_or(full(s, g), g == s)

            @pl.when(jnp.logical_not(jnp.logical_and(row == 0, has)))
            def _():
                act(in_plane(s, i))

    def forward(s):
        own_piece(s, lambda copy: copy.start())
        for q in range(groups):
            to_partner(s, q).start()

    def across(s, i, act):
        g = (s + i) % groups
        if s < g < stages:
            act(remote(
                half_ref(s, side), half_ref(s, side), half_send.at[i - 1],
                half_recv.at[s, side], (row, 2 * g + side),
            ))
        else:
            piece = side * groups + g
            act(remote(
                solved.at[s, piece], solved.at[s, piece], half_send.at[i - 1],
                piece_recv.at[s, piece], (row, 2 * g + side),
            ))

    @pl.when(early)
    def _():
        split_all()

    @pl.when(in_chain)
    def _():
        diag_copy().wait()
        for k in range(steps - 1):
            @pl.when(k < me)
            def _():
                strip_local(k).wait()

            @pl.when(k < 2 * group + 1 - side)
            def _():
                arrived(strip.at[1 - side, k], strip_recv.at[k])

        d0, d1 = diagonal[0], diagonal[1]
        d0_high, d0_low = halves(d0)
        below = strip[1, 2 * group]
        inner = product(below, d0_high, d0_low, NN)
        inner_high, inner_low = halves(inner)
        corner = -product(d1, inner_high, inner_low, NN)
        for r0, c0, value in (
            (0, 0, d0), (0, width, jnp.zeros_like(d0)), (width, 0, corner), (width, width, d1)
        ):
            h, l = halves(value)
            inverse_high[r0:r0 + width, c0:c0 + width] = h
            inverse_low[r0:r0 + width, c0:c0 + width] = l
        for s in range(stages - 1):
            @pl.when(s < group)
            def _():
                for b in range(2):
                    for t in range(2):
                        h, l = halves(strip[b, 2 * s + t])
                        place_ = (s, slice(b * width, (b + 1) * width), slice(t * width, (t + 1) * width))
                        strip_high[place_] = h
                        strip_low[place_] = l

        def first_wait(i, carry):
            arrived(first.at[i], first_recv.at[i])
            return carry

        lax.fori_loop(0, half_devices, first_wait, 0)

        def pile(i, carry):
            at = pl.ds(pl.multiple_of(i * 2 * local, 2 * local), 2 * local)
            for b in range(2):
                for t in range(width // 128):
                    lanes = slice(b * width + t * 128, b * width + (t + 1) * 128)
                    lead[at, lanes] = jnp.concatenate(
                        [first[2 * i, b, t], first[2 * i + 1, b, t]], axis=0
                    )
            return carry

        lax.fori_loop(0, half_devices // 2, pile, 0)

        for s in range(stages):
            @pl.when(s < group)
            def _():
                arrived(half_ref(s, side), half_recv.at[s, side])

                @pl.when(s + 1 < group)
                def _():
                    forward(s)

                x = half_ref(s, side)[...].reshape(half_count, 2 * width)
                lead[...] -= product(x, strip_high[min(s, stages - 2)], strip_low[min(s, stages - 2)], NT)

            @pl.when(s == group)
            def _():
                x = product(lead[...], inverse_high[...], inverse_low[...], NT)
                half_ref(s, side)[...] = x.reshape(groups, half_count // groups, 2 * width)
                for i in range(1, groups):
                    across(s, i, lambda copy: copy.start())
                if s > 0:
                    forward(s - 1)
                forward(s)
                if 2 * s < steps // 2:
                    send_rest()

    @pl.when(jnp.logical_not(early))
    def _():
        split_all()

    def holds(s):
        return jnp.logical_and(row == 0, jnp.logical_and(in_chain, s <= group))

    def pass_on(s):
        @pl.when(jnp.logical_not(holds(s)))
        def _():
            arrived(solved.at[s, mine], piece_recv.at[s, mine])
            own_piece(s, lambda copy: copy.start())
            to_partner(s, group).start()

    def update_with(s):
        @pl.when(jnp.logical_not(holds(s)))
        def _():
            for i in range(1, groups):
                q = (group + i) % groups
                piece = side * groups + q
                arrived(solved.at[s, piece], piece_recv.at[s, piece])
                to_partner(s, q).start()

        for q in range(groups):
            piece = (1 - side) * groups + q
            arrived(solved.at[s, piece], piece_recv.at[s, piece])

        x_high, x_low = halves(solved[s].reshape(count, 2 * width))
        both[:count] = x_high
        both[count:] = x_low

        def update(j, carry):
            a = mul(high[s, j], both[...], NT)
            b = mul(low[s, j], both[:count], NT)
            term = a[:, :count] + (a[:, count:] + b)
            if s == 0:
                total[j] = term
            elif s < stages - 1:
                total[j] += term
            else:
                out[j] -= term
            return carry

        lax.fori_loop(0, blocks, update, 0)

    for s in range(stages - 1):
        pass_on(s)
        update_with(s)
    pass_on(stages - 1)

    own_copy.wait()

    def a2a_wait(i, carry):
        source = (me + i) % devices

        @pl.when(in_chain)
        def _():
            arrived(recv.at[source, pl.ds(1, blocks - 1)], a2a_recv.at[source])

        @pl.when(jnp.logical_not(in_chain))
        def _():
            arrived(recv.at[source], a2a_recv.at[source])

        return carry

    lax.fori_loop(1, devices, a2a_wait, 0)

    def finish(j):
        def pile(i, carry):
            at = pl.ds(pl.multiple_of(i * 2 * local, 2 * local), 2 * local)
            for t in range(width // 128):
                piled[t, at] = jnp.concatenate([recv[2 * i, j, t], recv[2 * i + 1, j, t]], axis=0)
            return carry

        lax.fori_loop(0, half_devices, pile, 0)
        for t in range(width // 128):
            at = slice(t * 128, (t + 1) * 128)
            out[j, at] = piled[t].T - total[j, at]

    @pl.when(jnp.logical_not(in_chain))
    def _():
        finish(0)

    @pl.when(in_chain)
    def _():
        out[0] = jnp.zeros_like(out[0])

    for j in range(1, blocks):
        finish(j)

    update_with(stages - 1)

    @pl.when(in_chain)
    def _():
        for s in range(stages):
            for t in range(2):
                @pl.when(me == 2 * s + t)
                def _():
                    x = solved[s].reshape(count, 2 * width)
                    out[0] = x[:, t * width:(t + 1) * width].T

    for c in range(stages):
        @pl.when(2 * c + my_half != me)
        def _():
            first_remote(c).wait_send()

    @pl.when(in_chain)
    def _():
        for k in range(steps - 1):
            @pl.when(k < me)
            def _():
                strip_remote(k).wait_send()
        for s in range(stages):
            @pl.when(s == group)
            def _():
                for i in range(1, groups):
                    across(s, i, lambda copy: copy.wait_send())

    def a2a_sent(i, carry):
        target = (me + i) % devices

        @pl.when(target < steps)
        def _():
            a2a_lead(target).wait_send()

        @pl.when(target >= steps)
        def _():
            a2a_rest(target).wait_send()

        return carry

    lax.fori_loop(1, devices, a2a_sent, 0)
    for s in range(stages):
        own_piece(s, lambda copy: copy.wait_send())
        for q in range(groups):
            to_partner(s, q).wait_send()


def per_device(rows, cols, snapshots, panels, diag_inverse):
    local, order = snapshots.shape
    steps, blocks, width, _ = panels.shape
    devices = rows * cols
    groups = cols // 2
    stages = steps // 2
    count = local * devices
    lanes = 128
    snap = snapshots.reshape(local, blocks, devices, width // lanes, lanes).transpose(1, 2, 3, 0, 4)
    f32, bf16 = jnp.float32, jnp.bfloat16
    vmem, dma = pltpu.VMEM, pltpu.SemaphoreType.DMA
    return pl.pallas_call(
        functools.partial(kernel, rows, cols),
        out_shape=jax.ShapeDtypeStruct((blocks, width, count), f32),
        in_specs=[pl.BlockSpec(memory_space=pl.ANY)] * 3,
        out_specs=pl.BlockSpec(memory_space=pltpu.VMEM),
        scratch_shapes=[
            vmem((devices, blocks, width // lanes, local, lanes), f32),
            vmem((devices, blocks, width // lanes, local, lanes), f32),
            vmem((devices // 2, 2, width // lanes, local, lanes), f32),
            vmem((stages, cols, count // cols, 2 * width), f32),
            vmem((2, steps, width, width), f32),
            vmem((stages - 1, 2 * width, 2 * width), bf16),
            vmem((stages - 1, 2 * width, 2 * width), bf16),
            vmem((2 * width, 2 * width), bf16),
            vmem((2 * width, 2 * width), bf16),
            vmem((2, width, width), f32),
            vmem((count // 2, 2 * width), f32),
            vmem((steps, blocks, width, width), f32),
            vmem((stages, blocks, width, 2 * width), bf16),
            vmem((stages, blocks, width, 2 * width), bf16),
            vmem((2 * count, 2 * width), bf16),
            vmem((blocks, width, count), f32),
            vmem((width // lanes, count, lanes), f32),
            dma((devices,)), dma((devices,)),
            dma((stages,)), dma((devices // 2,)),
            dma((steps,)), dma((steps,)), dma((steps,)), dma(()),
            dma((steps,)),
            dma((groups,)), dma((stages, 2)), dma((stages, groups)), dma((stages,)),
            dma((stages, cols)), dma((stages, groups - 1)),
            dma((blocks,)),
        ],
        compiler_params=pltpu.CompilerParams(
            collective_id=0, has_side_effects=True, vmem_limit_bytes=58 * 1024 * 1024
        ),
        cost_estimate=pl.CostEstimate(
            flops=6 * steps * blocks * width * width * count,
            bytes_accessed=4 * steps * blocks * width * width,
            transcendentals=0,
        ),
    )(snap, panels, diag_inverse)


def solution(mesh):
    in_specs = (P(("row", "col"), None), P(None, None, ("row", "col"), None), P())
    out_specs = P(None, ("row", "col"), None)
    body = functools.partial(per_device, mesh.shape["row"], mesh.shape["col"])
    return jax.shard_map(
        body, mesh=mesh, in_specs=in_specs, out_specs=out_specs, check_vma=False
    )
```

```python
import functools

import jax
import jax.numpy as jnp
from jax import lax
from jax.experimental import pallas as pl
from jax.experimental.pallas import tpu as pltpu
from jax.sharding import PartitionSpec as P

MESH = pl.DeviceIdType.MESH
NT = (((1,), (1,)), ((), ()))
NN = (((1,), (0,)), ((), ()))


def halves(value):
    high = value.astype(jnp.bfloat16)
    low = (value - high.astype(jnp.float32)).astype(jnp.bfloat16)
    return high, low


def mul(a, b, dims):
    return lax.dot_general(a, b, dims, preferred_element_type=jnp.float32)


def product(a, b_high, b_low, dims):
    rows = a.shape[0]
    a_high, a_low = halves(a)
    both = mul(jnp.concatenate([a_high, a_low], axis=0), b_high, dims)
    return both[:rows] + (both[rows:] + mul(a_high, b_low, dims))


def kernel(
    rows, cols, snap, panels, diag, out,
    packed, recv, first, solved, strip, strip_high, strip_low, inverse_high, inverse_low,
    diagonal, lead, staged, high, low, both, total, piled,
    a2a_send, a2a_recv, first_send, first_recv, strip_send, strip_recv, strip_own, diag_sem,
    staged_sem, half_send, half_recv, partner_send, up_send, piece_recv, plane_send,
    pack_sem, swap_send, swap_recv,
):
    devices = rows * cols
    groups = cols // 2
    steps, blocks, width, _ = panels.shape
    stages = steps // 2
    count = out.shape[2]
    half_count = count // 2
    local = snap.shape[4]
    half_devices = devices // 2

    row = lax.axis_index("row")
    col = lax.axis_index("col")
    me = row * cols + col
    group = col // 2
    side = col % 2
    in_chain = me < steps

    def device(index):
        return (index // cols, index % cols)

    def remote(src, dst, send, recv_sem, target):
        return pltpu.make_async_remote_copy(
            src_ref=src, dst_ref=dst, send_sem=send, recv_sem=recv_sem,
            device_id=target, device_id_type=MESH,
        )

    def arrived(ref, sem):
        pltpu.make_async_copy(ref, ref, sem).wait()

    def strip_local(k):
        return pltpu.make_async_copy(panels.at[k, 0], strip.at[side, k], strip_own.at[k])

    def diag_copy():
        return pltpu.make_async_copy(diag.at[pl.ds(2 * group, 2)], diagonal, diag_sem)

    def staged_copy(k):
        return pltpu.make_async_copy(panels.at[k], staged.at[k], staged_sem.at[k])

    def pack(j):
        return pltpu.make_async_copy(
            snap.at[j, :, side], packed.at[j, :, side], pack_sem.at[j]
        )

    for j in range(blocks):
        pack(j).start()

    @pl.when(in_chain)
    def _():
        diag_copy().start()
        for k in range(steps - 1):
            @pl.when(k < me)
            def _():
                strip_local(k).start()

    barrier = pltpu.get_barrier_semaphore()

    def greet(i, carry):
        pl.semaphore_signal(
            barrier, inc=1, device_id=device((me + i) % devices), device_id_type=MESH
        )
        return carry

    lax.fori_loop(1, devices, greet, 0)
    pl.semaphore_wait(barrier, devices - 1)

    my_half = me // half_devices
    place = me % half_devices

    def first_remote(c):
        return remote(
            snap.at[0, c], first.at[place], first_send.at[c],
            first_recv.at[place], device(2 * c + my_half),
        )

    def first_local(c):
        return pltpu.make_async_copy(
            snap.at[0, c], first.at[place], first_recv.at[place]
        )

    for c in range(stages):
        @pl.when(2 * c + my_half != me)
        def _():
            first_remote(c).start()

        @pl.when(2 * c + my_half == me)
        def _():
            first_local(c).start()

    partner = (row, 2 * group + 1 - side)

    def strip_remote(k):
        return remote(
            panels.at[k, 0], strip.at[side, k], strip_send.at[k], strip_recv.at[k], partner
        )

    def strips():
        for k in reversed(range(steps - 1)):
            @pl.when(k < me)
            def _():
                strip_remote(k).start()

    @pl.when(me < 2)
    def _():
        strips()

    def swap(j):
        return remote(
            snap.at[j, :, 1 - side], packed.at[j, :, side], swap_send.at[j], swap_recv.at[j],
            partner,
        )

    for j in range(blocks):
        swap(j).start()

    @pl.when(jnp.logical_and(in_chain, me >= 2))
    def _():
        strips()

    for k in range(steps):
        staged_copy(k).start()

    pair = me // 2
    pairs = devices // 2

    def a2a_lead(to):
        return remote(
            packed.at[pl.ds(1, blocks - 1), to],
            recv.at[pl.ds(1, blocks - 1), pl.ds(2 * pair, 2)],
            a2a_send.at[to], a2a_recv.at[pair], device(2 * to + side),
        )

    def a2a_rest(to):
        return remote(
            packed.at[:, to], recv.at[:, pl.ds(2 * pair, 2)],
            a2a_send.at[to], a2a_recv.at[pair], device(2 * to + side),
        )

    own_copy = pltpu.make_async_copy(
        packed.at[:, pair], recv.at[:, pl.ds(2 * pair, 2)], a2a_recv.at[pair]
    )

    def a2a_start(i, carry):
        to = (pair + 1 + (i + pairs // 2 - groups // 2) % (pairs - 1)) % pairs

        @pl.when(2 * to < steps)
        def _():
            a2a_lead(to).start()

        @pl.when(2 * to >= steps)
        def _():
            a2a_rest(to).start()

        return carry

    def send_rest():
        for j in range(blocks):
            pack(j).wait()
            arrived(packed.at[j, :, 1 - side], swap_recv.at[j])
        lax.fori_loop(0, pairs - 1, a2a_start, 0)
        own_copy.start()

    waiting = me < steps // 2

    @pl.when(jnp.logical_not(waiting))
    def _():
        send_rest()

    def split_all():
        for k in range(steps):
            staged_copy(k).wait()

        def one(i, carry):
            s, j = i // blocks, i % blocks
            for t in range(2):
                h, l = halves(staged[2 * s + t, j])
                high[s, j, :, t * width:(t + 1) * width] = h
                low[s, j, :, t * width:(t + 1) * width] = l
            return carry

        lax.fori_loop(0, stages * blocks, one, 0)

    early = jnp.logical_or(me >= steps, me >= steps // 2)

    def half_ref(s, which):
        return solved.at[s, pl.ds(which * groups, groups)]

    mine = side * groups + group

    def full(s, g):
        return jnp.logical_and(g > s, g < stages)

    def to_partner(s, q):
        piece = side * groups + q
        return remote(
            solved.at[s, piece], solved.at[s, piece], partner_send.at[s, q],
            piece_recv.at[s, piece], partner,
        )

    def upward(s, r):
        return remote(
            solved.at[s, mine], solved.at[s, mine], up_send.at[s, r - 1],
            piece_recv.at[s, mine], (row + r, col),
        )

    def in_plane(s, i):
        g = (group + i) % groups
        return remote(
            solved.at[s, mine], solved.at[s, mine], plane_send.at[s, i - 1],
            piece_recv.at[s, mine], (row, 2 * g + side),
        )

    def own_piece(s, act):
        if s < stages - 1:
            @pl.when(row < rows - 1)
            def _():
                act(upward(s, 1))
        else:
            @pl.when(row == 0)
            def _():
                for r in range(1, rows):
                    act(upward(s, r))

        for i in range(1, groups):
            g = (group + i) % groups
            has = jnp.logical_or(full(s, g), g == s)

            @pl.when(jnp.logical_not(jnp.logical_and(row == 0, has)))
            def _():
                act(in_plane(s, i))

    def forward(s):
        own_piece(s, lambda copy: copy.start())
        for q in range(groups):
            to_partner(s, q).start()

    def across(s, i, act):
        g = (s + i) % groups
        if s < g < stages:
            act(remote(
                half_ref(s, side), half_ref(s, side), half_send.at[i - 1],
                half_recv.at[s, side], (row, 2 * g + side),
            ))
        else:
            piece = side * groups + g
            act(remote(
                solved.at[s, piece], solved.at[s, piece], half_send.at[i - 1],
                piece_recv.at[s, piece], (row, 2 * g + side),
            ))

    @pl.when(early)
    def _():
        split_all()

    @pl.when(in_chain)
    def _():
        diag_copy().wait()
        for k in range(steps - 1):
            @pl.when(k < me)
            def _():
                strip_local(k).wait()

            @pl.when(k < 2 * group + 1 - side)
            def _():
                arrived(strip.at[1 - side, k], strip_recv.at[k])

        d0, d1 = diagonal[0], diagonal[1]
        d0_high, d0_low = halves(d0)
        below = strip[1, 2 * group]
        inner = product(below, d0_high, d0_low, NN)
        inner_high, inner_low = halves(inner)
        corner = -product(d1, inner_high, inner_low, NN)
        for r0, c0, value in (
            (0, 0, d0), (0, width, jnp.zeros_like(d0)), (width, 0, corner), (width, width, d1)
        ):
            h, l = halves(value)
            inverse_high[r0:r0 + width, c0:c0 + width] = h
            inverse_low[r0:r0 + width, c0:c0 + width] = l
        for s in range(stages - 1):
            @pl.when(s < group)
            def _():
                for b in range(2):
                    for t in range(2):
                        h, l = halves(strip[b, 2 * s + t])
                        place_ = (s, slice(b * width, (b + 1) * width), slice(t * width, (t + 1) * width))
                        strip_high[place_] = h
                        strip_low[place_] = l

        def first_wait(i, carry):
            arrived(first.at[i], first_recv.at[i])
            return carry

        lax.fori_loop(0, half_devices, first_wait, 0)

        def pile(i, carry):
            at = pl.ds(pl.multiple_of(i * 2 * local, 2 * local), 2 * local)
            for b in range(2):
                for t in range(width // 128):
                    lanes = slice(b * width + t * 128, b * width + (t + 1) * 128)
                    lead[at, lanes] = jnp.concatenate(
                        [first[2 * i, b, t], first[2 * i + 1, b, t]], axis=0
                    )
            return carry

        lax.fori_loop(0, half_devices // 2, pile, 0)

        for s in range(stages):
            @pl.when(s < group)
            def _():
                arrived(half_ref(s, side), half_recv.at[s, side])

                @pl.when(s + 1 < group)
                def _():
                    forward(s)

                x = half_ref(s, side)[...].reshape(half_count, 2 * width)
                lead[...] -= product(x, strip_high[min(s, stages - 2)], strip_low[min(s, stages - 2)], NT)

            @pl.when(s == group)
            def _():
                x = product(lead[...], inverse_high[...], inverse_low[...], NT)
                half_ref(s, side)[...] = x.reshape(groups, half_count // groups, 2 * width)
                for i in range(1, groups):
                    across(s, i, lambda copy: copy.start())
                if s > 0:
                    forward(s - 1)
                forward(s)
                if 2 * s < steps // 2:
                    send_rest()

    @pl.when(jnp.logical_not(early))
    def _():
        split_all()

    def holds(s):
        return jnp.logical_and(row == 0, jnp.logical_and(in_chain, s <= group))

    def pass_on(s):
        @pl.when(jnp.logical_not(holds(s)))
        def _():
            arrived(solved.at[s, mine], piece_recv.at[s, mine])
            own_piece(s, lambda copy: copy.start())
            to_partner(s, group).start()

    def update_with(s):
        @pl.when(jnp.logical_not(holds(s)))
        def _():
            for i in range(1, groups):
                q = (group + i) % groups
                piece = side * groups + q
                arrived(solved.at[s, piece], piece_recv.at[s, piece])
                to_partner(s, q).start()

        for q in range(groups):
            piece = (1 - side) * groups + q
            arrived(solved.at[s, piece], piece_recv.at[s, piece])

        x_high, x_low = halves(solved[s].reshape(count, 2 * width))
        both[:count] = x_high
        both[count:] = x_low

        def update(j, carry):
            a = mul(high[s, j], both[...], NT)
            b = mul(low[s, j], both[:count], NT)
            term = a[:, :count] + (a[:, count:] + b)
            if s == 0:
                total[j] = term
            elif s < stages - 1:
                total[j] += term
            else:
                out[j] -= term
            return carry

        lax.fori_loop(0, blocks, update, 0)

    for s in range(stages - 1):
        pass_on(s)
        update_with(s)
    pass_on(stages - 1)

    own_copy.wait()

    def a2a_wait(i, carry):
        source = (pair + i) % pairs

        @pl.when(in_chain)
        def _():
            arrived(recv.at[pl.ds(1, blocks - 1), pl.ds(2 * source, 2)], a2a_recv.at[source])

        @pl.when(jnp.logical_not(in_chain))
        def _():
            arrived(recv.at[:, pl.ds(2 * source, 2)], a2a_recv.at[source])

        return carry

    lax.fori_loop(1, pairs, a2a_wait, 0)

    def finish(j):
        def pile(i, carry):
            at = pl.ds(pl.multiple_of(i * 2 * local, 2 * local), 2 * local)
            for t in range(width // 128):
                piled[t, at] = jnp.concatenate([recv[j, 2 * i, t], recv[j, 2 * i + 1, t]], axis=0)
            return carry

        lax.fori_loop(0, half_devices, pile, 0)
        for t in range(width // 128):
            at = slice(t * 128, (t + 1) * 128)
            out[j, at] = piled[t].T - total[j, at]

    @pl.when(jnp.logical_not(in_chain))
    def _():
        finish(0)

    @pl.when(in_chain)
    def _():
        out[0] = jnp.zeros_like(out[0])

    for j in range(1, blocks):
        finish(j)

    update_with(stages - 1)

    @pl.when(in_chain)
    def _():
        for s in range(stages):
            for t in range(2):
                @pl.when(me == 2 * s + t)
                def _():
                    x = solved[s].reshape(count, 2 * width)
                    out[0] = x[:, t * width:(t + 1) * width].T

    for c in range(stages):
        @pl.when(2 * c + my_half != me)
        def _():
            first_remote(c).wait_send()

    @pl.when(in_chain)
    def _():
        for k in range(steps - 1):
            @pl.when(k < me)
            def _():
                strip_remote(k).wait_send()
        for s in range(stages):
            @pl.when(s == group)
            def _():
                for i in range(1, groups):
                    across(s, i, lambda copy: copy.wait_send())

    def a2a_sent(i, carry):
        to = (pair + i) % pairs

        @pl.when(2 * to < steps)
        def _():
            a2a_lead(to).wait_send()

        @pl.when(2 * to >= steps)
        def _():
            a2a_rest(to).wait_send()

        return carry

    lax.fori_loop(1, pairs, a2a_sent, 0)
    for j in range(blocks):
        swap(j).wait_send()
    for s in range(stages):
        own_piece(s, lambda copy: copy.wait_send())
        for q in range(groups):
            to_partner(s, q).wait_send()


def per_device(rows, cols, snapshots, panels, diag_inverse):
    local, order = snapshots.shape
    steps, blocks, width, _ = panels.shape
    devices = rows * cols
    groups = cols // 2
    stages = steps // 2
    count = local * devices
    lanes = 128
    snap = snapshots.reshape(local, blocks, devices // 2, 2, width // lanes, lanes)
    snap = snap.transpose(1, 2, 3, 4, 0, 5)
    f32, bf16 = jnp.float32, jnp.bfloat16
    vmem, dma = pltpu.VMEM, pltpu.SemaphoreType.DMA
    return pl.pallas_call(
        functools.partial(kernel, rows, cols),
        out_shape=jax.ShapeDtypeStruct((blocks, width, count), f32),
        in_specs=[pl.BlockSpec(memory_space=pl.ANY)] * 3,
        out_specs=pl.BlockSpec(memory_space=pltpu.VMEM),
        scratch_shapes=[
            vmem((blocks, devices // 2, 2, width // lanes, local, lanes), f32),
            vmem((blocks, devices, width // lanes, local, lanes), f32),
            vmem((devices // 2, 2, width // lanes, local, lanes), f32),
            vmem((stages, cols, count // cols, 2 * width), f32),
            vmem((2, steps, width, width), f32),
            vmem((stages - 1, 2 * width, 2 * width), bf16),
            vmem((stages - 1, 2 * width, 2 * width), bf16),
            vmem((2 * width, 2 * width), bf16),
            vmem((2 * width, 2 * width), bf16),
            vmem((2, width, width), f32),
            vmem((count // 2, 2 * width), f32),
            vmem((steps, blocks, width, width), f32),
            vmem((stages, blocks, width, 2 * width), bf16),
            vmem((stages, blocks, width, 2 * width), bf16),
            vmem((2 * count, 2 * width), bf16),
            vmem((blocks, width, count), f32),
            vmem((width // lanes, count, lanes), f32),
            dma((devices // 2,)), dma((devices // 2,)),
            dma((stages,)), dma((devices // 2,)),
            dma((steps,)), dma((steps,)), dma((steps,)), dma(()),
            dma((steps,)),
            dma((groups,)), dma((stages, 2)), dma((stages, groups)), dma((stages, rows - 1)),
            dma((stages, cols)), dma((stages, groups - 1)),
            dma((blocks,)), dma((blocks,)), dma((blocks,)),
        ],
        compiler_params=pltpu.CompilerParams(
            collective_id=0, has_side_effects=True, vmem_limit_bytes=58 * 1024 * 1024
        ),
        cost_estimate=pl.CostEstimate(
            flops=6 * steps * blocks * width * width * count,
            bytes_accessed=4 * steps * blocks * width * width,
            transcendentals=0,
        ),
    )(snap, panels, diag_inverse)


def solution(mesh):
    in_specs = (P(("row", "col"), None), P(None, None, ("row", "col"), None), P())
    out_specs = P(None, ("row", "col"), None)
    body = functools.partial(per_device, mesh.shape["row"], mesh.shape["col"])
    return jax.shard_map(
        body, mesh=mesh, in_specs=in_specs, out_specs=out_specs, check_vma=False
    )
```

```python
import functools

import jax
import jax.numpy as jnp
from jax import lax
from jax.experimental import pallas as pl
from jax.experimental.pallas import tpu as pltpu
from jax.sharding import PartitionSpec as P

MESH = pl.DeviceIdType.MESH


def halves(value):
    high = value.astype(jnp.bfloat16)
    low = (value - high.astype(jnp.float32)).astype(jnp.bfloat16)
    return high, low


def mul(a, b):
    return jnp.dot(a, b, preferred_element_type=jnp.float32)


def product(a, b_high, b_low):
    rows = a.shape[0]
    a_high, a_low = halves(a)
    both = mul(jnp.concatenate([a_high, a_low], axis=0), b_high)
    return both[:rows] + (both[rows:] + mul(a_high, b_low))


def kernel(
    rows, cols, snap, panels, diag, out,
    packed, recv, first, solved, strip, strip_high, strip_low, inverse_high, inverse_low,
    diagonal, lead, staged, high, low, both, total,
    a2a_send, a2a_recv, first_send, first_recv, strip_send, strip_recv, strip_own, diag_sem,
    staged_sem, half_send, half_recv, partner_send, up_send, piece_recv, plane_send,
    pack_sem, swap_send, swap_recv,
):
    devices = rows * cols
    groups = cols // 2
    steps, blocks, width, _ = panels.shape
    stages = steps // 2
    count = out.shape[2]
    half_count = count // 2
    local = snap.shape[4]
    half_devices = devices // 2

    row = lax.axis_index("row")
    col = lax.axis_index("col")
    me = row * cols + col
    group = col // 2
    side = col % 2
    in_chain = me < steps

    def device(index):
        return (index // cols, index % cols)

    def remote(src, dst, send, recv_sem, target):
        return pltpu.make_async_remote_copy(
            src_ref=src, dst_ref=dst, send_sem=send, recv_sem=recv_sem,
            device_id=target, device_id_type=MESH,
        )

    def arrived(ref, sem):
        pltpu.make_async_copy(ref, ref, sem).wait()

    def strip_local(k):
        return pltpu.make_async_copy(panels.at[k, 0], strip.at[side, k], strip_own.at[k])

    def diag_copy():
        return pltpu.make_async_copy(diag.at[pl.ds(2 * group, 2)], diagonal, diag_sem)

    def staged_copy(k):
        return pltpu.make_async_copy(panels.at[k], staged.at[k], staged_sem.at[k])

    def pack(j):
        return pltpu.make_async_copy(
            snap.at[j, :, side], packed.at[j, :, side], pack_sem.at[j]
        )

    for j in range(blocks):
        pack(j).start()

    @pl.when(in_chain)
    def _():
        diag_copy().start()
        for k in range(steps - 1):
            @pl.when(k < me)
            def _():
                strip_local(k).start()

    barrier = pltpu.get_barrier_semaphore()

    def greet(i, carry):
        pl.semaphore_signal(
            barrier, inc=1, device_id=device((me + i) % devices), device_id_type=MESH
        )
        return carry

    lax.fori_loop(1, devices, greet, 0)
    pl.semaphore_wait(barrier, devices - 1)

    my_half = me // half_devices
    place = me % half_devices

    def first_remote(c):
        return remote(
            snap.at[0, c], first.at[place], first_send.at[c],
            first_recv.at[place], device(2 * c + my_half),
        )

    def first_local(c):
        return pltpu.make_async_copy(
            snap.at[0, c], first.at[place], first_recv.at[place]
        )

    for c in range(stages):
        @pl.when(2 * c + my_half != me)
        def _():
            first_remote(c).start()

        @pl.when(2 * c + my_half == me)
        def _():
            first_local(c).start()

    partner = (row, 2 * group + 1 - side)

    def strip_remote(k):
        return remote(
            panels.at[k, 0], strip.at[side, k], strip_send.at[k], strip_recv.at[k], partner
        )

    def strips():
        for k in reversed(range(steps - 1)):
            @pl.when(k < me)
            def _():
                strip_remote(k).start()

    @pl.when(me < 2)
    def _():
        strips()

    def swap(j):
        return remote(
            snap.at[j, :, 1 - side], packed.at[j, :, side], swap_send.at[j], swap_recv.at[j],
            partner,
        )

    for j in range(blocks):
        swap(j).start()

    @pl.when(jnp.logical_and(in_chain, me >= 2))
    def _():
        strips()

    for k in range(steps):
        staged_copy(k).start()

    pair = me // 2
    pairs = devices // 2

    def a2a_lead(to):
        return remote(
            packed.at[pl.ds(1, blocks - 1), to],
            recv.at[pl.ds(1, blocks - 1), pl.ds(2 * pair, 2)],
            a2a_send.at[to], a2a_recv.at[pair], device(2 * to + side),
        )

    def a2a_rest(to):
        return remote(
            packed.at[:, to], recv.at[:, pl.ds(2 * pair, 2)],
            a2a_send.at[to], a2a_recv.at[pair], device(2 * to + side),
        )

    own_copy = pltpu.make_async_copy(
        packed.at[:, pair], recv.at[:, pl.ds(2 * pair, 2)], a2a_recv.at[pair]
    )

    def a2a_start(i, carry):
        to = (pair + 1 + (i + pairs // 2 - groups // 2) % (pairs - 1)) % pairs

        @pl.when(2 * to < steps)
        def _():
            a2a_lead(to).start()

        @pl.when(2 * to >= steps)
        def _():
            a2a_rest(to).start()

        return carry

    def send_rest():
        for j in range(blocks):
            pack(j).wait()
            arrived(packed.at[j, :, 1 - side], swap_recv.at[j])
        lax.fori_loop(0, pairs - 1, a2a_start, 0)
        own_copy.start()

    waiting = me < steps // 2

    @pl.when(jnp.logical_not(waiting))
    def _():
        send_rest()

    def split_all():
        for k in range(steps):
            staged_copy(k).wait()

        def one(i, carry):
            s, j = i // blocks, i % blocks
            for t in range(2):
                h, l = halves(staged[2 * s + t, j])
                high[s, j, :, t * width:(t + 1) * width] = h
                low[s, j, :, t * width:(t + 1) * width] = l
            return carry

        lax.fori_loop(0, stages * blocks, one, 0)

    early = jnp.logical_or(me >= steps, me >= steps // 2)

    def half_ref(s, which):
        return solved.at[s, pl.ds(which * groups, groups)]

    mine = side * groups + group

    def full(s, g):
        return jnp.logical_and(g > s, g < stages)

    def to_partner(s, q):
        piece = side * groups + q
        return remote(
            solved.at[s, piece], solved.at[s, piece], partner_send.at[s, q],
            piece_recv.at[s, piece], partner,
        )

    def upward(s, r):
        return remote(
            solved.at[s, mine], solved.at[s, mine], up_send.at[s, r - 1],
            piece_recv.at[s, mine], (row + r, col),
        )

    def in_plane(s, i):
        g = (group + i) % groups
        return remote(
            solved.at[s, mine], solved.at[s, mine], plane_send.at[s, i - 1],
            piece_recv.at[s, mine], (row, 2 * g + side),
        )

    def own_piece(s, act):
        @pl.when(row == 0)
        def _():
            for r in range(1, rows):
                act(upward(s, r))

        for i in range(1, groups):
            g = (group + i) % groups
            has = jnp.logical_or(full(s, g), g == s)

            @pl.when(jnp.logical_not(jnp.logical_and(row == 0, has)))
            def _():
                act(in_plane(s, i))

    def forward(s):
        own_piece(s, lambda copy: copy.start())
        for q in range(groups):
            to_partner(s, q).start()

    def across(s, i, act):
        g = (s + i) % groups
        if s < g < stages:
            act(remote(
                half_ref(s, side), half_ref(s, side), half_send.at[i - 1],
                half_recv.at[s, side], (row, 2 * g + side),
            ))
        else:
            piece = side * groups + g
            act(remote(
                solved.at[s, piece], solved.at[s, piece], half_send.at[i - 1],
                piece_recv.at[s, piece], (row, 2 * g + side),
            ))

    @pl.when(early)
    def _():
        split_all()

    @pl.when(in_chain)
    def _():
        diag_copy().wait()
        for k in range(steps - 1):
            @pl.when(k < me)
            def _():
                strip_local(k).wait()

            @pl.when(k < 2 * group + 1 - side)
            def _():
                arrived(strip.at[1 - side, k], strip_recv.at[k])

        d0, d1 = diagonal[0], diagonal[1]
        d0_high, d0_low = halves(d0)
        below = strip[1, 2 * group]
        inner = product(below, d0_high, d0_low)
        inner_high, inner_low = halves(inner)
        corner = -product(d1, inner_high, inner_low)
        for r0, c0, value in (
            (0, 0, d0.T), (width, 0, jnp.zeros_like(d0)), (0, width, corner.T), (width, width, d1.T)
        ):
            h, l = halves(value)
            inverse_high[r0:r0 + width, c0:c0 + width] = h
            inverse_low[r0:r0 + width, c0:c0 + width] = l
        for s in range(stages - 1):
            @pl.when(s < group)
            def _():
                for b in range(2):
                    for t in range(2):
                        h, l = halves(strip[b, 2 * s + t].T)
                        place_ = (s, slice(t * width, (t + 1) * width), slice(b * width, (b + 1) * width))
                        strip_high[place_] = h
                        strip_low[place_] = l

        def first_wait(i, carry):
            arrived(first.at[i], first_recv.at[i])
            return carry

        lax.fori_loop(0, half_devices, first_wait, 0)

        for b in range(2):
            for t in range(width // 128):
                lanes = slice(b * width + t * 128, b * width + (t + 1) * 128)
                lead[:, lanes] = first[:, b, t].reshape(half_count, 128)

        for s in range(stages):
            @pl.when(s < group)
            def _():
                arrived(half_ref(s, side), half_recv.at[s, side])

                @pl.when(s + 1 < group)
                def _():
                    forward(s)

                x = half_ref(s, side)[...].reshape(half_count, 2 * width)
                lead[...] -= product(x, strip_high[min(s, stages - 2)], strip_low[min(s, stages - 2)])

            @pl.when(s == group)
            def _():
                x = product(lead[...], inverse_high[...], inverse_low[...])
                half_ref(s, side)[...] = x.reshape(groups, half_count // groups, 2 * width)
                for i in range(1, groups):
                    across(s, i, lambda copy: copy.start())
                if s > 0:
                    forward(s - 1)
                forward(s)
                if 2 * s < steps // 2:
                    send_rest()

    @pl.when(jnp.logical_not(early))
    def _():
        split_all()

    def holds(s):
        return jnp.logical_and(row == 0, jnp.logical_and(in_chain, s <= group))

    def pass_on(s):
        @pl.when(jnp.logical_not(holds(s)))
        def _():
            arrived(solved.at[s, mine], piece_recv.at[s, mine])
            own_piece(s, lambda copy: copy.start())
            to_partner(s, group).start()

    def update_with(s):
        @pl.when(jnp.logical_not(holds(s)))
        def _():
            for i in range(1, groups):
                q = (group + i) % groups
                piece = side * groups + q
                arrived(solved.at[s, piece], piece_recv.at[s, piece])
                to_partner(s, q).start()

        for q in range(groups):
            piece = (1 - side) * groups + q
            arrived(solved.at[s, piece], piece_recv.at[s, piece])

        x_high, x_low = halves(solved[s].reshape(count, 2 * width).T)
        both[:, :count] = x_high
        both[:, count:] = x_low

        def update(i, carry):
            j = pl.ds(2 * i, 2)
            a = mul(high[s, j].reshape(2 * width, 2 * width), both[...])
            b = mul(low[s, j].reshape(2 * width, 2 * width), both[:, :count])
            term = (a[:, :count] + (a[:, count:] + b)).reshape(2, width, count)
            if s == 0:
                total[j] = term
            elif s < stages - 1:
                total[j] += term
            else:
                out[j] -= term
            return carry

        lax.fori_loop(0, blocks // 2, update, 0)

    for s in range(stages - 1):
        pass_on(s)
        update_with(s)
    pass_on(stages - 1)

    own_copy.wait()

    def a2a_wait(i, carry):
        source = (pair + i) % pairs

        @pl.when(in_chain)
        def _():
            arrived(recv.at[pl.ds(1, blocks - 1), pl.ds(2 * source, 2)], a2a_recv.at[source])

        @pl.when(jnp.logical_not(in_chain))
        def _():
            arrived(recv.at[:, pl.ds(2 * source, 2)], a2a_recv.at[source])

        return carry

    lax.fori_loop(1, pairs, a2a_wait, 0)

    def finish(j):
        for t in range(width // 128):
            at = slice(t * 128, (t + 1) * 128)
            out[j, at] = recv[j, :, t].reshape(count, 128).T - total[j, at]

    @pl.when(jnp.logical_not(in_chain))
    def _():
        finish(0)

    @pl.when(in_chain)
    def _():
        out[0] = jnp.zeros_like(out[0])

    for j in range(1, blocks):
        finish(j)

    update_with(stages - 1)

    @pl.when(in_chain)
    def _():
        for s in range(stages):
            for t in range(2):
                @pl.when(me == 2 * s + t)
                def _():
                    x = solved[s].reshape(count, 2 * width)
                    out[0] = x[:, t * width:(t + 1) * width].T

    for c in range(stages):
        @pl.when(2 * c + my_half != me)
        def _():
            first_remote(c).wait_send()

    @pl.when(in_chain)
    def _():
        for k in range(steps - 1):
            @pl.when(k < me)
            def _():
                strip_remote(k).wait_send()
        for s in range(stages):
            @pl.when(s == group)
            def _():
                for i in range(1, groups):
                    across(s, i, lambda copy: copy.wait_send())

    def a2a_sent(i, carry):
        to = (pair + i) % pairs

        @pl.when(2 * to < steps)
        def _():
            a2a_lead(to).wait_send()

        @pl.when(2 * to >= steps)
        def _():
            a2a_rest(to).wait_send()

        return carry

    lax.fori_loop(1, pairs, a2a_sent, 0)
    for j in range(blocks):
        swap(j).wait_send()
    for s in range(stages):
        own_piece(s, lambda copy: copy.wait_send())
        for q in range(groups):
            to_partner(s, q).wait_send()


def per_device(rows, cols, snapshots, panels, diag_inverse):
    local, order = snapshots.shape
    steps, blocks, width, _ = panels.shape
    devices = rows * cols
    groups = cols // 2
    stages = steps // 2
    count = local * devices
    lanes = 128
    snap = snapshots.reshape(local, blocks, devices // 2, 2, width // lanes, lanes)
    snap = snap.transpose(1, 2, 3, 4, 0, 5)
    f32, bf16 = jnp.float32, jnp.bfloat16
    vmem, dma = pltpu.VMEM, pltpu.SemaphoreType.DMA
    return pl.pallas_call(
        functools.partial(kernel, rows, cols),
        out_shape=jax.ShapeDtypeStruct((blocks, width, count), f32),
        in_specs=[pl.BlockSpec(memory_space=pl.ANY)] * 3,
        out_specs=pl.BlockSpec(memory_space=pltpu.VMEM),
        scratch_shapes=[
            vmem((blocks, devices // 2, 2, width // lanes, local, lanes), f32),
            vmem((blocks, devices, width // lanes, local, lanes), f32),
            vmem((devices // 2, 2, width // lanes, local, lanes), f32),
            vmem((stages, cols, count // cols, 2 * width), f32),
            vmem((2, steps, width, width), f32),
            vmem((stages - 1, 2 * width, 2 * width), bf16),
            vmem((stages - 1, 2 * width, 2 * width), bf16),
            vmem((2 * width, 2 * width), bf16),
            vmem((2 * width, 2 * width), bf16),
            vmem((2, width, width), f32),
            vmem((count // 2, 2 * width), f32),
            vmem((steps, blocks, width, width), f32),
            vmem((stages, blocks, width, 2 * width), bf16),
            vmem((stages, blocks, width, 2 * width), bf16),
            vmem((2 * width, 2 * count), bf16),
            vmem((blocks, width, count), f32),
            dma((devices // 2,)), dma((devices // 2,)),
            dma((stages,)), dma((devices // 2,)),
            dma((steps,)), dma((steps,)), dma((steps,)), dma(()),
            dma((steps,)),
            dma((groups,)), dma((stages, 2)), dma((stages, groups)), dma((stages, rows - 1)),
            dma((stages, cols)), dma((stages, groups - 1)),
            dma((blocks,)), dma((blocks,)), dma((blocks,)),
        ],
        compiler_params=pltpu.CompilerParams(
            collective_id=0, has_side_effects=True, vmem_limit_bytes=58 * 1024 * 1024
        ),
        cost_estimate=pl.CostEstimate(
            flops=6 * steps * blocks * width * width * count,
            bytes_accessed=4 * steps * blocks * width * width,
            transcendentals=0,
        ),
    )(snap, panels, diag_inverse)


def solution(mesh):
    in_specs = (P(("row", "col"), None), P(None, None, ("row", "col"), None), P())
    out_specs = P(None, ("row", "col"), None)
    body = functools.partial(per_device, mesh.shape["row"], mesh.shape["col"])
    return jax.shard_map(
        body, mesh=mesh, in_specs=in_specs, out_specs=out_specs, check_vma=False
    )
```

```python
import functools

import jax
import jax.numpy as jnp
from jax import lax
from jax.experimental import pallas as pl
from jax.experimental.pallas import tpu as pltpu
from jax.sharding import PartitionSpec as P

MESH = pl.DeviceIdType.MESH


def halves(value):
    high = value.astype(jnp.bfloat16)
    low = (value - high.astype(jnp.float32)).astype(jnp.bfloat16)
    return high, low


def mul(a, b):
    return jnp.dot(a, b, preferred_element_type=jnp.float32)


def product(a, b_high, b_low):
    rows = a.shape[0]
    a_high, a_low = halves(a)
    both = mul(jnp.concatenate([a_high, a_low], axis=0), b_high)
    return both[:rows] + (both[rows:] + mul(a_high, b_low))


def kernel(
    rows, cols, snap, panels, diag, out,
    packed, recv, first, solved, strip, strip_high, strip_low, inverse_high, inverse_low,
    diagonal, lead, staged, high, low, both, total,
    a2a_send, a2a_recv, first_send, first_recv, strip_send, strip_recv, strip_own, diag_sem,
    staged_sem, half_send, half_recv, partner_send, up_send, piece_recv, plane_send,
    pack_sem, swap_send, swap_recv,
):
    devices = rows * cols
    groups = cols // 2
    steps, blocks, width, _ = panels.shape
    stages = steps // 2
    count = out.shape[2]
    half_count = count // 2
    local = snap.shape[4]
    half_devices = devices // 2

    row = lax.axis_index("row")
    col = lax.axis_index("col")
    me = row * cols + col
    group = col // 2
    side = col % 2
    in_chain = me < steps

    def device(index):
        return (index // cols, index % cols)

    def remote(src, dst, send, recv_sem, target):
        return pltpu.make_async_remote_copy(
            src_ref=src, dst_ref=dst, send_sem=send, recv_sem=recv_sem,
            device_id=target, device_id_type=MESH,
        )

    def arrived(ref, sem):
        pltpu.make_async_copy(ref, ref, sem).wait()

    def strip_local(k):
        return pltpu.make_async_copy(panels.at[k, 0], strip.at[side, k], strip_own.at[k])

    def diag_copy():
        return pltpu.make_async_copy(diag.at[pl.ds(2 * group, 2)], diagonal, diag_sem)

    def staged_copy(k):
        return pltpu.make_async_copy(panels.at[k], staged.at[k], staged_sem.at[k])

    def pack(j):
        return pltpu.make_async_copy(
            snap.at[j, :, side], packed.at[j, :, side], pack_sem.at[j]
        )

    for j in range(blocks):
        pack(j).start()

    @pl.when(in_chain)
    def _():
        diag_copy().start()
        for k in range(steps - 1):
            @pl.when(k < me)
            def _():
                strip_local(k).start()

    barrier = pltpu.get_barrier_semaphore()

    def greet(i, carry):
        pl.semaphore_signal(
            barrier, inc=1, device_id=device((me + i) % devices), device_id_type=MESH
        )
        return carry

    lax.fori_loop(1, devices, greet, 0)
    pl.semaphore_wait(barrier, devices - 1)

    my_half = me // half_devices
    place = me % half_devices

    def first_remote(c):
        return remote(
            snap.at[0, c], first.at[place], first_send.at[c],
            first_recv.at[place], device(2 * c + my_half),
        )

    def first_local(c):
        return pltpu.make_async_copy(
            snap.at[0, c], first.at[place], first_recv.at[place]
        )

    for c in range(stages):
        @pl.when(2 * c + my_half != me)
        def _():
            first_remote(c).start()

        @pl.when(2 * c + my_half == me)
        def _():
            first_local(c).start()

    partner = (row, 2 * group + 1 - side)

    def strip_remote(k):
        return remote(
            panels.at[k, 0], strip.at[side, k], strip_send.at[k], strip_recv.at[k], partner
        )

    def strips():
        for k in reversed(range(steps - 1)):
            @pl.when(k < me)
            def _():
                strip_remote(k).start()

    @pl.when(me < 2)
    def _():
        strips()

    def swap(j):
        return remote(
            snap.at[j, :, 1 - side], packed.at[j, :, side], swap_send.at[j], swap_recv.at[j],
            partner,
        )

    for j in range(blocks):
        swap(j).start()

    @pl.when(jnp.logical_and(in_chain, me >= 2))
    def _():
        strips()

    for k in range(steps):
        staged_copy(k).start()

    pair = me // 2
    pairs = devices // 2

    def a2a_lead(to):
        return remote(
            packed.at[pl.ds(1, blocks - 1), to],
            recv.at[pl.ds(1, blocks - 1), pl.ds(2 * pair, 2)],
            a2a_send.at[to], a2a_recv.at[pair], device(2 * to + side),
        )

    def a2a_rest(to):
        return remote(
            packed.at[:, to], recv.at[:, pl.ds(2 * pair, 2)],
            a2a_send.at[to], a2a_recv.at[pair], device(2 * to + side),
        )

    own_copy = pltpu.make_async_copy(
        packed.at[:, pair], recv.at[:, pl.ds(2 * pair, 2)], a2a_recv.at[pair]
    )

    def a2a_start(i, carry):
        to = (pair + 1 + (i + pairs // 2 - groups // 2) % (pairs - 1)) % pairs

        @pl.when(2 * to < steps)
        def _():
            a2a_lead(to).start()

        @pl.when(2 * to >= steps)
        def _():
            a2a_rest(to).start()

        return carry

    def swapped():
        for j in range(blocks):
            pack(j).wait()
            arrived(packed.at[j, :, 1 - side], swap_recv.at[j])
        own_copy.start()

    others = pairs - 1
    opening = jnp.where(in_chain, others // 5, 4 * others // 15)
    until = [(7 + 3 * s) * others // 15 for s in range(stages - 1)] + [others]

    def batch(begin, end):
        lax.fori_loop(begin, end, a2a_start, 0)

    leads = jnp.logical_and(in_chain, group == 0)
    opening = jnp.where(leads, 0, opening)

    @pl.when(jnp.logical_not(leads))
    def _():
        swapped()
        batch(0, opening)

    def split_all():
        for k in range(steps):
            staged_copy(k).wait()

        def one(i, carry):
            s, j = i // blocks, i % blocks
            for t in range(2):
                h, l = halves(staged[2 * s + t, j])
                high[s, j, :, t * width:(t + 1) * width] = h
                low[s, j, :, t * width:(t + 1) * width] = l
            return carry

        lax.fori_loop(0, stages * blocks, one, 0)

    early = jnp.logical_or(me >= steps, me >= steps // 2)

    def half_ref(s, which):
        return solved.at[s, pl.ds(which * groups, groups)]

    mine = side * groups + group

    def full(s, g):
        return jnp.logical_and(g > s, g < stages)

    def to_partner(s, q):
        piece = side * groups + q
        return remote(
            solved.at[s, piece], solved.at[s, piece], partner_send.at[s, q],
            piece_recv.at[s, piece], partner,
        )

    def upward(s, r):
        return remote(
            solved.at[s, mine], solved.at[s, mine], up_send.at[s, r - 1],
            piece_recv.at[s, mine], (row + r, col),
        )

    def in_plane(s, i):
        g = (group + i) % groups
        return remote(
            solved.at[s, mine], solved.at[s, mine], plane_send.at[s, i - 1],
            piece_recv.at[s, mine], (row, 2 * g + side),
        )

    def own_piece(s, act):
        @pl.when(row == 0)
        def _():
            for r in range(1, rows):
                act(upward(s, r))

        for i in range(1, groups):
            g = (group + i) % groups
            has = jnp.logical_or(full(s, g), g == s)

            @pl.when(jnp.logical_not(jnp.logical_and(row == 0, has)))
            def _():
                act(in_plane(s, i))

    def forward(s):
        own_piece(s, lambda copy: copy.start())
        for q in range(groups):
            to_partner(s, q).start()

    def across(s, i, act):
        g = (s + i) % groups
        if s < g < stages:
            act(remote(
                half_ref(s, side), half_ref(s, side), half_send.at[i - 1],
                half_recv.at[s, side], (row, 2 * g + side),
            ))
        else:
            piece = side * groups + g
            act(remote(
                solved.at[s, piece], solved.at[s, piece], half_send.at[i - 1],
                piece_recv.at[s, piece], (row, 2 * g + side),
            ))

    @pl.when(early)
    def _():
        split_all()

    @pl.when(in_chain)
    def _():
        diag_copy().wait()
        for k in range(steps - 1):
            @pl.when(k < me)
            def _():
                strip_local(k).wait()

            @pl.when(k < 2 * group + 1 - side)
            def _():
                arrived(strip.at[1 - side, k], strip_recv.at[k])

        d0, d1 = diagonal[0], diagonal[1]
        d0_high, d0_low = halves(d0)
        below = strip[1, 2 * group]
        inner = product(below, d0_high, d0_low)
        inner_high, inner_low = halves(inner)
        corner = -product(d1, inner_high, inner_low)
        for r0, c0, value in (
            (0, 0, d0.T), (width, 0, jnp.zeros_like(d0)), (0, width, corner.T), (width, width, d1.T)
        ):
            h, l = halves(value)
            inverse_high[r0:r0 + width, c0:c0 + width] = h
            inverse_low[r0:r0 + width, c0:c0 + width] = l
        for s in range(stages - 1):
            @pl.when(s < group)
            def _():
                for b in range(2):
                    for t in range(2):
                        h, l = halves(strip[b, 2 * s + t].T)
                        place_ = (s, slice(t * width, (t + 1) * width), slice(b * width, (b + 1) * width))
                        strip_high[place_] = h
                        strip_low[place_] = l

        def first_wait(i, carry):
            arrived(first.at[i], first_recv.at[i])
            return carry

        lax.fori_loop(0, half_devices, first_wait, 0)

        for b in range(2):
            for t in range(width // 128):
                lanes = slice(b * width + t * 128, b * width + (t + 1) * 128)
                lead[:, lanes] = first[:, b, t].reshape(half_count, 128)

        for s in range(stages):
            @pl.when(s < group)
            def _():
                arrived(half_ref(s, side), half_recv.at[s, side])

                @pl.when(s + 1 < group)
                def _():
                    forward(s)

                x = half_ref(s, side)[...].reshape(half_count, 2 * width)
                lead[...] -= product(x, strip_high[min(s, stages - 2)], strip_low[min(s, stages - 2)])

            @pl.when(s == group)
            def _():
                x = product(lead[...], inverse_high[...], inverse_low[...])
                half_ref(s, side)[...] = x.reshape(groups, half_count // groups, 2 * width)
                for i in range(1, groups):
                    across(s, i, lambda copy: copy.start())
                if s > 0:
                    forward(s - 1)
                forward(s)
                if s == 0:
                    swapped()
                batch(opening, until[0])

    @pl.when(jnp.logical_not(early))
    def _():
        split_all()

    def holds(s):
        return jnp.logical_and(row == 0, jnp.logical_and(in_chain, s <= group))

    def pass_on(s):
        @pl.when(jnp.logical_not(holds(s)))
        def _():
            arrived(solved.at[s, mine], piece_recv.at[s, mine])
            own_piece(s, lambda copy: copy.start())
            to_partner(s, group).start()

    def update_with(s):
        @pl.when(jnp.logical_not(holds(s)))
        def _():
            for i in range(1, groups):
                q = (group + i) % groups
                piece = side * groups + q
                arrived(solved.at[s, piece], piece_recv.at[s, piece])
                to_partner(s, q).start()

        for q in range(groups):
            piece = (1 - side) * groups + q
            arrived(solved.at[s, piece], piece_recv.at[s, piece])

        x_high, x_low = halves(solved[s].reshape(count, 2 * width).T)
        both[:, :count] = x_high
        both[:, count:] = x_low

        def update(i, carry):
            j = pl.ds(2 * i, 2)
            a = mul(high[s, j].reshape(2 * width, 2 * width), both[...])
            b = mul(low[s, j].reshape(2 * width, 2 * width), both[:, :count])
            term = (a[:, :count] + (a[:, count:] + b)).reshape(2, width, count)
            if s == 0:
                total[j] = term
            elif s < stages - 1:
                total[j] += term
            else:
                out[j] -= term
            return carry

        lax.fori_loop(0, blocks // 2, update, 0)

    for s in range(stages):
        pass_on(s)
        if s == 0:
            @pl.when(jnp.logical_not(in_chain))
            def _():
                batch(opening, until[0])
        else:
            batch(until[s - 1], until[s])
        if s < stages - 1:
            update_with(s)

    own_copy.wait()

    def a2a_wait(i, carry):
        source = (pair + i) % pairs

        @pl.when(in_chain)
        def _():
            arrived(recv.at[pl.ds(1, blocks - 1), pl.ds(2 * source, 2)], a2a_recv.at[source])

        @pl.when(jnp.logical_not(in_chain))
        def _():
            arrived(recv.at[:, pl.ds(2 * source, 2)], a2a_recv.at[source])

        return carry

    lax.fori_loop(1, pairs, a2a_wait, 0)

    def finish(j):
        for t in range(width // 128):
            at = slice(t * 128, (t + 1) * 128)
            out[j, at] = recv[j, :, t].reshape(count, 128).T - total[j, at]

    @pl.when(jnp.logical_not(in_chain))
    def _():
        finish(0)

    @pl.when(in_chain)
    def _():
        out[0] = jnp.zeros_like(out[0])

    for j in range(1, blocks):
        finish(j)

    update_with(stages - 1)

    @pl.when(in_chain)
    def _():
        for s in range(stages):
            for t in range(2):
                @pl.when(me == 2 * s + t)
                def _():
                    x = solved[s].reshape(count, 2 * width)
                    out[0] = x[:, t * width:(t + 1) * width].T

    for c in range(stages):
        @pl.when(2 * c + my_half != me)
        def _():
            first_remote(c).wait_send()

    @pl.when(in_chain)
    def _():
        for k in range(steps - 1):
            @pl.when(k < me)
            def _():
                strip_remote(k).wait_send()
        for s in range(stages):
            @pl.when(s == group)
            def _():
                for i in range(1, groups):
                    across(s, i, lambda copy: copy.wait_send())

    def a2a_sent(i, carry):
        to = (pair + i) % pairs

        @pl.when(2 * to < steps)
        def _():
            a2a_lead(to).wait_send()

        @pl.when(2 * to >= steps)
        def _():
            a2a_rest(to).wait_send()

        return carry

    lax.fori_loop(1, pairs, a2a_sent, 0)
    for j in range(blocks):
        swap(j).wait_send()
    for s in range(stages):
        own_piece(s, lambda copy: copy.wait_send())
        for q in range(groups):
            to_partner(s, q).wait_send()


def per_device(rows, cols, snapshots, panels, diag_inverse):
    local, order = snapshots.shape
    steps, blocks, width, _ = panels.shape
    devices = rows * cols
    groups = cols // 2
    stages = steps // 2
    count = local * devices
    lanes = 128
    snap = snapshots.reshape(local, blocks, devices // 2, 2, width // lanes, lanes)
    snap = snap.transpose(1, 2, 3, 4, 0, 5)
    f32, bf16 = jnp.float32, jnp.bfloat16
    vmem, dma = pltpu.VMEM, pltpu.SemaphoreType.DMA
    return pl.pallas_call(
        functools.partial(kernel, rows, cols),
        out_shape=jax.ShapeDtypeStruct((blocks, width, count), f32),
        in_specs=[pl.BlockSpec(memory_space=pl.ANY)] * 3,
        out_specs=pl.BlockSpec(memory_space=pltpu.VMEM),
        scratch_shapes=[
            vmem((blocks, devices // 2, 2, width // lanes, local, lanes), f32),
            vmem((blocks, devices, width // lanes, local, lanes), f32),
            vmem((devices // 2, 2, width // lanes, local, lanes), f32),
            vmem((stages, cols, count // cols, 2 * width), f32),
            vmem((2, steps, width, width), f32),
            vmem((stages - 1, 2 * width, 2 * width), bf16),
            vmem((stages - 1, 2 * width, 2 * width), bf16),
            vmem((2 * width, 2 * width), bf16),
            vmem((2 * width, 2 * width), bf16),
            vmem((2, width, width), f32),
            vmem((count // 2, 2 * width), f32),
            vmem((steps, blocks, width, width), f32),
            vmem((stages, blocks, width, 2 * width), bf16),
            vmem((stages, blocks, width, 2 * width), bf16),
            vmem((2 * width, 2 * count), bf16),
            vmem((blocks, width, count), f32),
            dma((devices // 2,)), dma((devices // 2,)),
            dma((stages,)), dma((devices // 2,)),
            dma((steps,)), dma((steps,)), dma((steps,)), dma(()),
            dma((steps,)),
            dma((groups,)), dma((stages, 2)), dma((stages, groups)), dma((stages, rows - 1)),
            dma((stages, cols)), dma((stages, groups - 1)),
            dma((blocks,)), dma((blocks,)), dma((blocks,)),
        ],
        compiler_params=pltpu.CompilerParams(
            collective_id=0, has_side_effects=True, vmem_limit_bytes=58 * 1024 * 1024
        ),
        cost_estimate=pl.CostEstimate(
            flops=6 * steps * blocks * width * width * count,
            bytes_accessed=4 * steps * blocks * width * width,
            transcendentals=0,
        ),
    )(snap, panels, diag_inverse)


def solution(mesh):
    in_specs = (P(("row", "col"), None), P(None, None, ("row", "col"), None), P())
    out_specs = P(None, ("row", "col"), None)
    body = functools.partial(per_device, mesh.shape["row"], mesh.shape["col"])
    return jax.shard_map(
        body, mesh=mesh, in_specs=in_specs, out_specs=out_specs, check_vma=False
    )
```

```python
import functools

import jax
import jax.numpy as jnp
from jax import lax
from jax.experimental import pallas as pl
from jax.experimental.pallas import tpu as pltpu
from jax.sharding import PartitionSpec as P

MESH = pl.DeviceIdType.MESH


def halves(value):
    high = value.astype(jnp.bfloat16)
    low = (value - high.astype(jnp.float32)).astype(jnp.bfloat16)
    return high, low


def mul(a, b):
    return jnp.dot(a, b, preferred_element_type=jnp.float32)


def product(a, b_high, b_low):
    rows = a.shape[0]
    a_high, a_low = halves(a)
    both = mul(jnp.concatenate([a_high, a_low], axis=0), b_high)
    return both[:rows] + (both[rows:] + mul(a_high, b_low))


def kernel(
    rows, cols, snap, panels, diag, out,
    packed, recv, first, solved, strip, strip_high, strip_low, inverse_high, inverse_low,
    diagonal, lead, staged, high, low, both, total,
    a2a_send, a2a_recv, first_send, first_recv, strip_send, strip_recv, strip_own, diag_sem,
    staged_sem, half_send, half_recv, partner_send, up_send, piece_recv, plane_send,
    pack_sem, swap_send, swap_recv,
):
    devices = rows * cols
    groups = cols // 2
    steps, blocks, width, _ = panels.shape
    stages = steps // 2
    count = out.shape[2]
    half_count = count // 2
    local = snap.shape[4]
    half_devices = devices // 2

    row = lax.axis_index("row")
    col = lax.axis_index("col")
    me = row * cols + col
    group = col // 2
    side = col % 2
    in_chain = me < steps

    def device(index):
        return (index // cols, index % cols)

    def remote(src, dst, send, recv_sem, target):
        return pltpu.make_async_remote_copy(
            src_ref=src, dst_ref=dst, send_sem=send, recv_sem=recv_sem,
            device_id=target, device_id_type=MESH,
        )

    def arrived(ref, sem):
        pltpu.make_async_copy(ref, ref, sem).wait()

    def strip_local(k):
        return pltpu.make_async_copy(panels.at[k, 0], strip.at[side, k], strip_own.at[k])

    def diag_copy():
        return pltpu.make_async_copy(diag.at[pl.ds(2 * group, 2)], diagonal, diag_sem)

    def staged_copy(k):
        return pltpu.make_async_copy(panels.at[k], staged.at[k], staged_sem.at[k])

    def pack(j):
        return pltpu.make_async_copy(
            snap.at[j, :, side], packed.at[j, :, side], pack_sem.at[j]
        )

    for j in range(blocks):
        pack(j).start()

    @pl.when(in_chain)
    def _():
        diag_copy().start()
        for k in range(steps - 1):
            @pl.when(k < me)
            def _():
                strip_local(k).start()

    barrier = pltpu.get_barrier_semaphore()

    def greet(i, carry):
        pl.semaphore_signal(
            barrier, inc=1, device_id=device((me + i) % devices), device_id_type=MESH
        )
        return carry

    lax.fori_loop(1, devices, greet, 0)
    pl.semaphore_wait(barrier, devices - 1)

    my_half = me // half_devices
    place = me % half_devices

    def first_remote(c):
        return remote(
            snap.at[0, c], first.at[place], first_send.at[c],
            first_recv.at[place], device(2 * c + my_half),
        )

    def first_local(c):
        return pltpu.make_async_copy(
            snap.at[0, c], first.at[place], first_recv.at[place]
        )

    for c in range(stages):
        @pl.when(2 * c + my_half != me)
        def _():
            first_remote(c).start()

        @pl.when(2 * c + my_half == me)
        def _():
            first_local(c).start()

    partner = (row, 2 * group + 1 - side)

    def strip_remote(k):
        return remote(
            panels.at[k, 0], strip.at[side, k], strip_send.at[k], strip_recv.at[k], partner
        )

    def strips():
        for k in reversed(range(steps - 1)):
            @pl.when(k < me)
            def _():
                strip_remote(k).start()

    @pl.when(me < 2)
    def _():
        strips()

    def swap(j):
        return remote(
            snap.at[j, :, 1 - side], packed.at[j, :, side], swap_send.at[j], swap_recv.at[j],
            partner,
        )

    for j in range(blocks):
        swap(j).start()

    @pl.when(jnp.logical_and(in_chain, me >= 2))
    def _():
        strips()

    for k in range(steps):
        staged_copy(k).start()

    pair = me // 2
    pairs = devices // 2

    def a2a_lead(to):
        return remote(
            packed.at[pl.ds(1, blocks - 1), to],
            recv.at[pl.ds(1, blocks - 1), pl.ds(2 * pair, 2)],
            a2a_send.at[to], a2a_recv.at[pair], device(2 * to + side),
        )

    def a2a_rest(to):
        return remote(
            packed.at[:, to], recv.at[:, pl.ds(2 * pair, 2)],
            a2a_send.at[to], a2a_recv.at[pair], device(2 * to + side),
        )

    own_copy = pltpu.make_async_copy(
        packed.at[:, pair], recv.at[:, pl.ds(2 * pair, 2)], a2a_recv.at[pair]
    )

    def a2a_start(i, carry):
        to = (pair + 1 + (i + pairs // 2 - groups // 2) % (pairs - 1)) % pairs

        @pl.when(2 * to < steps)
        def _():
            a2a_lead(to).start()

        @pl.when(2 * to >= steps)
        def _():
            a2a_rest(to).start()

        return carry

    def swapped():
        for j in range(blocks):
            pack(j).wait()
            arrived(packed.at[j, :, 1 - side], swap_recv.at[j])
        own_copy.start()

    others = pairs - 1
    leads = me < steps // 2
    opening = jnp.where(leads, 0, jnp.where(in_chain, (others + 1) // 2, others))

    def batch(begin, end):
        lax.fori_loop(begin, end, a2a_start, 0)

    @pl.when(jnp.logical_not(leads))
    def _():
        swapped()
        batch(0, opening)

    def split_all():
        for k in range(steps):
            staged_copy(k).wait()

        def one(i, carry):
            s, j = i // blocks, i % blocks
            for t in range(2):
                h, l = halves(staged[2 * s + t, j])
                high[s, j, :, t * width:(t + 1) * width] = h
                low[s, j, :, t * width:(t + 1) * width] = l
            return carry

        lax.fori_loop(0, stages * blocks, one, 0)

    early = jnp.logical_or(me >= steps, me >= steps // 2)

    def half_ref(s, which):
        return solved.at[s, pl.ds(which * groups, groups)]

    mine = side * groups + group

    def full(s, g):
        return jnp.logical_and(g > s, g < stages)

    def to_partner(s, q):
        piece = side * groups + q
        return remote(
            solved.at[s, piece], solved.at[s, piece], partner_send.at[s, q],
            piece_recv.at[s, piece], partner,
        )

    def upward(s, r):
        return remote(
            solved.at[s, mine], solved.at[s, mine], up_send.at[s, r - 1],
            piece_recv.at[s, mine], (row + r, col),
        )

    def in_plane(s, i):
        g = (group + i) % groups
        return remote(
            solved.at[s, mine], solved.at[s, mine], plane_send.at[s, i - 1],
            piece_recv.at[s, mine], (row, 2 * g + side),
        )

    def own_piece(s, act):
        @pl.when(row == 0)
        def _():
            for r in range(1, rows):
                act(upward(s, r))

        for i in range(1, groups):
            g = (group + i) % groups
            has = jnp.logical_or(full(s, g), g == s)

            @pl.when(jnp.logical_not(jnp.logical_and(row == 0, has)))
            def _():
                act(in_plane(s, i))

    def forward(s):
        own_piece(s, lambda copy: copy.start())
        for q in range(groups):
            to_partner(s, q).start()

    def across(s, i, act):
        g = (s + i) % groups
        if s < g < stages:
            act(remote(
                half_ref(s, side), half_ref(s, side), half_send.at[i - 1],
                half_recv.at[s, side], (row, 2 * g + side),
            ))
        else:
            piece = side * groups + g
            act(remote(
                solved.at[s, piece], solved.at[s, piece], half_send.at[i - 1],
                piece_recv.at[s, piece], (row, 2 * g + side),
            ))

    @pl.when(early)
    def _():
        split_all()

    @pl.when(in_chain)
    def _():
        diag_copy().wait()
        for k in range(steps - 1):
            @pl.when(k < me)
            def _():
                strip_local(k).wait()

            @pl.when(k < 2 * group + 1 - side)
            def _():
                arrived(strip.at[1 - side, k], strip_recv.at[k])

        d0, d1 = diagonal[0], diagonal[1]
        d0_high, d0_low = halves(d0)
        below = strip[1, 2 * group]
        inner = product(below, d0_high, d0_low)
        inner_high, inner_low = halves(inner)
        corner = -product(d1, inner_high, inner_low)
        for r0, c0, value in (
            (0, 0, d0.T), (width, 0, jnp.zeros_like(d0)), (0, width, corner.T), (width, width, d1.T)
        ):
            h, l = halves(value)
            inverse_high[r0:r0 + width, c0:c0 + width] = h
            inverse_low[r0:r0 + width, c0:c0 + width] = l
        for s in range(stages - 1):
            @pl.when(s < group)
            def _():
                for b in range(2):
                    for t in range(2):
                        h, l = halves(strip[b, 2 * s + t].T)
                        place_ = (s, slice(t * width, (t + 1) * width), slice(b * width, (b + 1) * width))
                        strip_high[place_] = h
                        strip_low[place_] = l

        def first_wait(i, carry):
            arrived(first.at[i], first_recv.at[i])
            return carry

        lax.fori_loop(0, half_devices, first_wait, 0)

        for b in range(2):
            for t in range(width // 128):
                lanes = slice(b * width + t * 128, b * width + (t + 1) * 128)
                lead[:, lanes] = first[:, b, t].reshape(half_count, 128)

        for s in range(stages):
            @pl.when(s < group)
            def _():
                arrived(half_ref(s, side), half_recv.at[s, side])

                @pl.when(s + 1 < group)
                def _():
                    forward(s)

                x = half_ref(s, side)[...].reshape(half_count, 2 * width)
                lead[...] -= product(x, strip_high[min(s, stages - 2)], strip_low[min(s, stages - 2)])

            @pl.when(s == group)
            def _():
                x = product(lead[...], inverse_high[...], inverse_low[...])
                half_ref(s, side)[...] = x.reshape(groups, half_count // groups, 2 * width)
                for i in range(1, groups):
                    across(s, i, lambda copy: copy.start())
                if s > 0:
                    forward(s - 1)
                forward(s)
                if 2 * s < steps // 2:
                    swapped()
                batch(opening, others)

    @pl.when(jnp.logical_not(early))
    def _():
        split_all()

    def holds(s):
        return jnp.logical_and(row == 0, jnp.logical_and(in_chain, s <= group))

    def pass_on(s):
        @pl.when(jnp.logical_not(holds(s)))
        def _():
            arrived(solved.at[s, mine], piece_recv.at[s, mine])
            own_piece(s, lambda copy: copy.start())
            to_partner(s, group).start()

    def update_with(s):
        @pl.when(jnp.logical_not(holds(s)))
        def _():
            for i in range(1, groups):
                q = (group + i) % groups
                piece = side * groups + q
                arrived(solved.at[s, piece], piece_recv.at[s, piece])
                to_partner(s, q).start()

        for q in range(groups):
            piece = (1 - side) * groups + q
            arrived(solved.at[s, piece], piece_recv.at[s, piece])

        x_high, x_low = halves(solved[s].reshape(count, 2 * width).T)
        both[:, :count] = x_high
        both[:, count:] = x_low

        def update(i, carry):
            j = pl.ds(2 * i, 2)
            a = mul(high[s, j].reshape(2 * width, 2 * width), both[...])
            b = mul(low[s, j].reshape(2 * width, 2 * width), both[:, :count])
            term = (a[:, :count] + (a[:, count:] + b)).reshape(2, width, count)
            if s == 0:
                total[j] = term
            elif s < stages - 1:
                total[j] += term
            else:
                out[j] -= term
            return carry

        lax.fori_loop(0, blocks // 2, update, 0)

    for s in range(stages):
        pass_on(s)
        if s < stages - 1:
            update_with(s)

    own_copy.wait()

    def a2a_wait(i, carry):
        source = (pair + i) % pairs

        @pl.when(in_chain)
        def _():
            arrived(recv.at[pl.ds(1, blocks - 1), pl.ds(2 * source, 2)], a2a_recv.at[source])

        @pl.when(jnp.logical_not(in_chain))
        def _():
            arrived(recv.at[:, pl.ds(2 * source, 2)], a2a_recv.at[source])

        return carry

    lax.fori_loop(1, pairs, a2a_wait, 0)

    def finish(j):
        for t in range(width // 128):
            at = slice(t * 128, (t + 1) * 128)
            out[j, at] = recv[j, :, t].reshape(count, 128).T - total[j, at]

    @pl.when(jnp.logical_not(in_chain))
    def _():
        finish(0)

    @pl.when(in_chain)
    def _():
        out[0] = jnp.zeros_like(out[0])

    for j in range(1, blocks):
        finish(j)

    update_with(stages - 1)

    @pl.when(in_chain)
    def _():
        for s in range(stages):
            for t in range(2):
                @pl.when(me == 2 * s + t)
                def _():
                    x = solved[s].reshape(count, 2 * width)
                    out[0] = x[:, t * width:(t + 1) * width].T

    for c in range(stages):
        @pl.when(2 * c + my_half != me)
        def _():
            first_remote(c).wait_send()

    @pl.when(in_chain)
    def _():
        for k in range(steps - 1):
            @pl.when(k < me)
            def _():
                strip_remote(k).wait_send()
        for s in range(stages):
            @pl.when(s == group)
            def _():
                for i in range(1, groups):
                    across(s, i, lambda copy: copy.wait_send())

    def a2a_sent(i, carry):
        to = (pair + i) % pairs

        @pl.when(2 * to < steps)
        def _():
            a2a_lead(to).wait_send()

        @pl.when(2 * to >= steps)
        def _():
            a2a_rest(to).wait_send()

        return carry

    lax.fori_loop(1, pairs, a2a_sent, 0)
    for j in range(blocks):
        swap(j).wait_send()
    for s in range(stages):
        own_piece(s, lambda copy: copy.wait_send())
        for q in range(groups):
            to_partner(s, q).wait_send()


def per_device(rows, cols, snapshots, panels, diag_inverse):
    local, order = snapshots.shape
    steps, blocks, width, _ = panels.shape
    devices = rows * cols
    groups = cols // 2
    stages = steps // 2
    count = local * devices
    lanes = 128
    snap = snapshots.reshape(local, blocks, devices // 2, 2, width // lanes, lanes)
    snap = snap.transpose(1, 2, 3, 4, 0, 5)
    f32, bf16 = jnp.float32, jnp.bfloat16
    vmem, dma = pltpu.VMEM, pltpu.SemaphoreType.DMA
    return pl.pallas_call(
        functools.partial(kernel, rows, cols),
        out_shape=jax.ShapeDtypeStruct((blocks, width, count), f32),
        in_specs=[pl.BlockSpec(memory_space=pl.ANY)] * 3,
        out_specs=pl.BlockSpec(memory_space=pltpu.VMEM),
        scratch_shapes=[
            vmem((blocks, devices // 2, 2, width // lanes, local, lanes), f32),
            vmem((blocks, devices, width // lanes, local, lanes), f32),
            vmem((devices // 2, 2, width // lanes, local, lanes), f32),
            vmem((stages, cols, count // cols, 2 * width), f32),
            vmem((2, steps, width, width), f32),
            vmem((stages - 1, 2 * width, 2 * width), bf16),
            vmem((stages - 1, 2 * width, 2 * width), bf16),
            vmem((2 * width, 2 * width), bf16),
            vmem((2 * width, 2 * width), bf16),
            vmem((2, width, width), f32),
            vmem((count // 2, 2 * width), f32),
            vmem((steps, blocks, width, width), f32),
            vmem((stages, blocks, width, 2 * width), bf16),
            vmem((stages, blocks, width, 2 * width), bf16),
            vmem((2 * width, 2 * count), bf16),
            vmem((blocks, width, count), f32),
            dma((devices // 2,)), dma((devices // 2,)),
            dma((stages,)), dma((devices // 2,)),
            dma((steps,)), dma((steps,)), dma((steps,)), dma(()),
            dma((steps,)),
            dma((groups,)), dma((stages, 2)), dma((stages, groups)), dma((stages, rows - 1)),
            dma((stages, cols)), dma((stages, groups - 1)),
            dma((blocks,)), dma((blocks,)), dma((blocks,)),
        ],
        compiler_params=pltpu.CompilerParams(
            collective_id=0, has_side_effects=True, vmem_limit_bytes=58 * 1024 * 1024
        ),
        cost_estimate=pl.CostEstimate(
            flops=6 * steps * blocks * width * width * count,
            bytes_accessed=4 * steps * blocks * width * width,
            transcendentals=0,
        ),
    )(snap, panels, diag_inverse)


def solution(mesh):
    in_specs = (P(("row", "col"), None), P(None, None, ("row", "col"), None), P())
    out_specs = P(None, ("row", "col"), None)
    body = functools.partial(per_device, mesh.shape["row"], mesh.shape["col"])
    return jax.shard_map(
        body, mesh=mesh, in_specs=in_specs, out_specs=out_specs, check_vma=False
    )
```
